256 devices in a mesh: grp: 8 (over z), dp: 32 (over y, x, core).
Axes of the slice: x: 4, y: 4, z: 8, core: 2. Of those that a mesh axis runs over, the one named last changes fastest.
Arguments:
- attn: bfloat16 [131072, 2048], P(('grp', 'dp')), may hold values from -6 to 6
- hidden: bfloat16 [131072, 4096], P(('grp', 'dp')), may hold values from -6 to 6
- output_weight_rows: bfloat16 [2048, 4096], P('dp'), may hold values from -0.125 to 0.125
- down_factor: bfloat16 [2048, 16], replicated, may hold values from -0.125 to 0.125
- up_factor: bfloat16 [16, 4096], replicated, may hold values from -1.5 to 1.5
- final_norm_gain: float32 [4096], replicated, may hold values from 0.5 to 1.5
- queries: bfloat16 [512, 4096], P(('grp', 'dp')), may hold values from -6 to 6
- lengths: int32 [512], P(('grp', 'dp')), may hold values from 32 to 256
- offsets: int32 [512], P(('grp', 'dp')), may hold values from 0 to 256, as said below
- positives: int32 [512], P(('grp', 'dp')), may hold values from 0 to 511, as said below
Outputs:
- attention_gradient: bfloat16 [131072, 2048], P(('grp', 'dp'))
- query_gradient: float32 [512, 4096], P(('grp', 'dp'))
- down_factor_gradient: float32 [2048, 16], replicated
- up_factor_gradient: float32 [16, 4096], replicated
- loss: float32 [], replicated
The draws below stay inside these ranges and needn't reach their ends.
Inputs may be any that keep to these rules, and one draw needn't show every extreme that they name: `offsets`: within each block of 2 passages the first offset is 0 and each next offset is the previous one plus the previous length rounded up to a multiple of 64; the last passage ends within the block's 512 rows. `positives`: each passage is the positive of exactly one query.
All inputs are finite; a program needn't handle non-finite values.
Results may differ from the reference program's by a relative error of at most 0.0077.
Values may be sent and summed in bfloat16 or wider, within the bound.
A program may use at most 128 MiB of HBM per device.

```python
import jax
import jax.numpy as jnp
from jax import lax

MODEL_WIDTH = 4096
HEAD_FEATURES = 2048
ADAPTER_RANK = 16
TOK_DEV = 512
PAS_DEV = 2
MAXLEN = 256
MINLEN = 32
BUCKET = 64
PASSAGES = 512
TOKENS = 131072
N_GRP = 8
N_DP = 32


def passage_plan(key):
    spans = jax.random.randint(key, (PASSAGES,), MINLEN, MAXLEN + 1)
    blocks = PASSAGES // PAS_DEV
    picks = jax.random.randint(jax.random.fold_in(key, 11), (2,), 0, blocks)
    chosen = picks[0]
    other = (chosen + 1 + picks[1] % (blocks - 1)) % blocks
    places = jnp.arange(PASSAGES, dtype=jnp.int32)
    in_chosen = places // PAS_DEV == chosen
    local = places % PAS_DEV
    spans = jnp.where(in_chosen & (local < PAS_DEV - 1), MAXLEN, spans)
    spans = jnp.where(in_chosen & (local == PAS_DEV - 1), MINLEN, spans)
    spans = jnp.where(places == other * PAS_DEV, MAXLEN, spans)
    return spans.astype(jnp.int32)


def passage_topics(key):
    base = jax.random.normal(jax.random.fold_in(key, 21), (PASSAGES, MODEL_WIDTH), jnp.float32)
    twist = jax.random.normal(jax.random.fold_in(key, 22), (PASSAGES, MODEL_WIDTH), jnp.float32)
    return (base, twist)


def pairing(key):
    return jax.random.permutation(jax.random.fold_in(key, 23), PASSAGES).astype(jnp.int32)


def draw_lengths(key, part):
    spans = passage_plan(key)
    return spans


def draw_offsets(key, part):
    spans = passage_plan(key)
    padded = (spans + BUCKET - 1) // BUCKET * BUCKET
    per_device = padded.reshape(-1, PAS_DEV)
    starts = jnp.cumsum(per_device, axis=1) - per_device
    return starts.reshape(-1).astype(jnp.int32)


def draw_positives(key, part):
    matched = pairing(key)
    return matched


def draw_hidden(key, part):
    spans = passage_plan(key)
    base, twist = passage_topics(key)
    key = jax.random.fold_in(key, 3)
    blocks = PASSAGES // PAS_DEV
    padded = (spans + BUCKET - 1) // BUCKET * BUCKET
    per_device = padded.reshape(-1, PAS_DEV)
    starts = jnp.cumsum(per_device, axis=1) - per_device
    span_blocks = spans.reshape(-1, PAS_DEV)
    local = jnp.arange(TOK_DEV, dtype=jnp.int32)
    inside = (local[None, :, None] >= starts[:, None, :]) & (local[None, :, None] < starts[:, None, :] + span_blocks[:, None, :])
    slot = jnp.sum(inside.astype(jnp.int32) * jnp.arange(PAS_DEV, dtype=jnp.int32)[None, None, :], axis=-1)
    valid = jnp.any(inside, axis=-1).astype(jnp.float32).reshape(-1, 1)
    owner = (jnp.arange(blocks, dtype=jnp.int32)[:, None] * PAS_DEV + slot).reshape(-1)
    rows = jnp.arange(TOKENS, dtype=jnp.int32)
    sign = (1 - 2 * (rows % 2)).astype(jnp.float32)[:, None]
    magnitude = jax.random.uniform(jax.random.fold_in(key, 31), (TOKENS, 1), jnp.float32, 0.8, 1.2)
    noise = jax.random.normal(jax.random.fold_in(key, 32), (TOKENS, MODEL_WIDTH), jnp.float32)
    scale = jnp.ones((TOKENS, 1), jnp.float32)
    topical = jnp.take(base, owner, axis=0) + sign * magnitude * jnp.take(twist, owner, axis=0)
    values = 0.55 * scale * (valid * topical + 0.5 * noise)
    return jnp.clip(values, -6.0, 6.0).astype(jnp.bfloat16)


def draw_queries(key, part):
    base, twist = passage_topics(key)
    matched = pairing(key)
    key = jax.random.fold_in(key, 5)
    noise = jax.random.normal(jax.random.fold_in(key, 41), (PASSAGES, MODEL_WIDTH), jnp.float32)
    values = (jnp.take(base, matched, axis=0) + 5.0 * jnp.take(twist, matched, axis=0) + 4.5 * noise) / 7.0
    return jnp.clip(values, -6.0, 6.0).astype(jnp.bfloat16)


def block_scale(key, dims, cuts, smallest, largest):
    loudness = 1.0
    for position, parts in cuts:
        steps = jax.random.uniform(jax.random.fold_in(jax.random.fold_in(key, 6), position), (parts,), jnp.float32, smallest / len(cuts), largest / len(cuts))
        loudness = loudness * jnp.repeat(jnp.exp(steps), dims[position] // parts).reshape((-1,) + (1,) * (len(dims) - 1 - position))
    return loudness


def bell_draw(own_key, shape, width, reach, cuts=(), held_as=jnp.bfloat16):
    gain = block_scale(own_key, shape, cuts, -0.22, 0.18) if cuts else 1.0
    array = jax.random.normal(own_key, shape, jnp.float32) * width * gain
    return jnp.minimum(jnp.maximum(array, -reach), reach).astype(held_as)


def setup_inputs(seed: int = 0) -> dict:
    arg_keys = jax.random.split(jax.random.key(seed), 11)
    return {
        "attn": bell_draw(arg_keys[0], (TOKENS, HEAD_FEATURES), 1.0, 6.0, ((0, 256),)),
        "hidden": draw_hidden(jax.random.fold_in(arg_keys[10], 71), 0),
        "output_weight_rows": bell_draw(arg_keys[2], (HEAD_FEATURES, MODEL_WIDTH), HEAD_FEATURES ** -0.5, 0.125, ((0, 32),)),
        "down_factor": bell_draw(arg_keys[3], (HEAD_FEATURES, ADAPTER_RANK), HEAD_FEATURES ** -0.5, 0.125),
        "up_factor": bell_draw(arg_keys[4], (ADAPTER_RANK, MODEL_WIDTH), ADAPTER_RANK ** -0.5, 1.5),
        "final_norm_gain": jnp.clip(1.0 + 0.1 * jax.random.normal(arg_keys[5], (MODEL_WIDTH,), jnp.float32), 0.5, 1.5),
        "queries": draw_queries(jax.random.fold_in(arg_keys[10], 71), 0),
        "lengths": draw_lengths(jax.random.fold_in(arg_keys[10], 71), 0),
        "offsets": draw_offsets(jax.random.fold_in(arg_keys[10], 71), 0),
        "positives": draw_positives(jax.random.fold_in(arg_keys[10], 71), 0),
    }


def pool_block(hidden_block, offset_block, length_block, final_norm_gain):
    values = hidden_block.astype(jnp.float32)
    rstd = lax.rsqrt(lax.optimization_barrier(jnp.mean(values * values, axis=-1, keepdims=True)) + 1e-05)
    normed = values * rstd
    shaped = normed * final_norm_gain
    rows = jnp.arange(values.shape[0], dtype=jnp.int32)
    inside = (rows[None, :] >= offset_block[:, None]) & (rows[None, :] < offset_block[:, None] + length_block[:, None])
    member = inside.astype(jnp.float32)
    counts = length_block.astype(jnp.float32)[:, None]
    pooled = jnp.dot(member, shaped, precision=lax.Precision.HIGHEST) / counts
    return (pooled, member, counts, rstd, normed)

def reference(attn, hidden, output_weight_rows, down_factor, up_factor, final_norm_gain, queries, lengths, offsets, positives):
    devices = N_GRP * N_DP
    total = PAS_DEV * devices
    hidden_blocks = hidden.reshape(devices, TOK_DEV, MODEL_WIDTH)
    attn_blocks = attn.reshape(devices, TOK_DEV, HEAD_FEATURES)
    offset_blocks = offsets.reshape(devices, PAS_DEV)
    length_blocks = lengths.reshape(devices, PAS_DEV)

    def forward_one(items):
        pooled, member, counts, rstd, normed = pool_block(items[0], items[1], items[2], final_norm_gain)
        return pooled
    pooled = lax.map(forward_one, (hidden_blocks, offset_blocks, length_blocks)).reshape(total, MODEL_WIDTH)
    pnorm = jnp.sqrt(lax.optimization_barrier(jnp.sum(pooled * pooled, axis=-1, keepdims=True)) + 1e-06)
    embed = pooled / pnorm
    embed_b = embed.astype(jnp.bfloat16)
    query_f = queries.astype(jnp.float32)
    qnorm = jnp.sqrt(lax.optimization_barrier(jnp.sum(query_f * query_f, axis=-1, keepdims=True)) + 1e-06)
    unit = query_f / qnorm
    unit_b = unit.astype(jnp.bfloat16)
    logits = 50.0 * jnp.dot(unit_b, embed_b.T, preferred_element_type=jnp.float32)
    lse = jnp.log(lax.optimization_barrier(jnp.sum(jnp.exp(logits), axis=-1)))
    prob = jnp.exp(logits - lse[:, None])
    target = (positives[:, None] == jnp.arange(total, dtype=jnp.int32)[None, :]).astype(jnp.float32)
    loss = jnp.mean(lse - lax.optimization_barrier(jnp.sum(logits * target, axis=-1)))
    grad = ((prob - target) * 1024.0).astype(jnp.bfloat16)
    d_unit = 50.0 * jnp.dot(grad, embed_b, preferred_element_type=jnp.float32)
    d_embed = 50.0 * jnp.dot(grad.T, unit_b, preferred_element_type=jnp.float32)
    query_gradient = (d_unit - unit * lax.optimization_barrier(jnp.sum(unit * d_unit, axis=-1, keepdims=True))) / qnorm
    d_pooled = (d_embed - embed * lax.optimization_barrier(jnp.sum(embed * d_embed, axis=-1, keepdims=True))) / pnorm
    d_pooled_blocks = d_pooled.reshape(devices, PAS_DEV, MODEL_WIDTH)

    def backward_one(items):
        hidden_block, attention_slice, offset_block, length_block, d_block = items
        pooled_b, member, counts, rstd, normed = pool_block(hidden_block, offset_block, length_block, final_norm_gain)
        dz = jnp.dot(member.T, d_block / counts, precision=lax.Precision.HIGHEST)
        dn = dz * final_norm_gain
        output_gradient = (rstd * (dn - normed * lax.optimization_barrier(jnp.mean(dn * normed, axis=-1, keepdims=True)))).astype(jnp.bfloat16)
        backward_lower = (2.0 * jnp.dot(output_gradient, up_factor.T, preferred_element_type=jnp.float32)).astype(jnp.bfloat16)
        forward_lower = jnp.dot(attention_slice, down_factor, preferred_element_type=jnp.float32).astype(jnp.bfloat16)
        frozen_product = jnp.dot(output_gradient, output_weight_rows.T, preferred_element_type=jnp.float32)
        attention_slice_gradient = (frozen_product + jnp.dot(backward_lower, down_factor.T, preferred_element_type=jnp.float32)).astype(jnp.bfloat16)
        down_factor_piece = jnp.dot(attention_slice.T, backward_lower, preferred_element_type=jnp.float32)
        up_factor_piece = 2.0 * jnp.dot(forward_lower.T, output_gradient, preferred_element_type=jnp.float32)
        return (attention_slice_gradient, down_factor_piece, up_factor_piece)
    d_attn_blocks, down_factor_pieces, up_factor_pieces = lax.map(backward_one, (hidden_blocks, attn_blocks, offset_blocks, length_blocks, d_pooled_blocks))
    attention_gradient = d_attn_blocks.reshape(devices * TOK_DEV, HEAD_FEATURES)
    down_factor_gradient = lax.optimization_barrier(jnp.sum(down_factor_pieces, axis=0))
    up_factor_gradient = lax.optimization_barrier(jnp.sum(up_factor_pieces, axis=0))
    return (attention_gradient, query_gradient, down_factor_gradient, up_factor_gradient, loss)
```

```python
import functools

import jax
import jax.numpy as jnp
from jax import lax
from jax.experimental import pallas as pl
from jax.experimental.pallas import tpu as pltpu
from jax.sharding import PartitionSpec as P

MESH = pl.DeviceIdType.MESH
F32 = jnp.float32
BF16 = jnp.bfloat16
HI = lax.Precision.HIGHEST
NT = (((1,), (1,)), ((), ()))
TN = (((0,), (0,)), ((), ()))


def iota(shape, dim):
    return lax.broadcasted_iota(jnp.int32, shape, dim)


def mm(a, b, dims=None, precision=None):
    if dims is None:
        dims = (((1,), (0,)), ((), ()))
    return lax.dot_general(a, b, dims, precision=precision, preferred_element_type=F32)


def split3(x):
    high = x.astype(BF16).astype(F32)
    rest = x - high
    mid = rest.astype(BF16).astype(F32)
    return high, mid, (rest - mid).astype(BF16).astype(F32)


def kernel(
    ng,
    nq,
    hidden,
    attn,
    down_t,
    up,
    gain,
    queries,
    lengths,
    offsets,
    positives,
    dy_out,
    blt_out,
    query_out,
    adapter_out,
    loss_out,
    hv,
    av,
    dyv,
    ub,
    eb,
    unit_s,
    pool_s,
    ssq_s,
    col_s,
    dn_s,
    lx,
    dpb,
    rb,
    dub,
    rub,
    ab,
    core_in,
    plane_in,
    z_in,
    total_s,
    local_sem,
    u_send,
    u_recv,
    e_send,
    e_recv,
    x_send,
    x_recv,
    d_send,
    d_recv,
    v_send,
    v_recv,
    c_send,
    c_recv,
    p_send,
    p_recv,
    z_send,
    z_recv,
    g_send,
    g_recv,
    s_send,
    s_recv,
):
    nl = 2 * ng
    tok, width = hv.shape
    wc = width // 8
    feat = av.shape[1]
    passages = 2 * nl * nq
    grp = lax.axis_index("grp")
    dp = lax.axis_index("dp")
    core = lax.rem(dp, 2)
    q_me = lax.div(dp, 2)
    l_me = 2 * grp + core

    def plane_peer(o):
        q = lax.rem(q_me + o, nq)
        return q, (grp, 2 * q + core)

    def line_peer(o):
        l = lax.rem(l_me + o, nl)
        return l, (lax.div(l, 2), 2 * q_me + lax.rem(l, 2))

    def z_peer(o):
        z = lax.rem(grp + o, ng)
        return z, (z, dp)

    def fan_out(n, peer, source, target, me, send, recv):
        def body(o, carry):
            there, device = peer(o)
            pltpu.make_async_remote_copy(
                src_ref=source(there),
                dst_ref=target.at[me],
                send_sem=send.at[there],
                recv_sem=recv.at[me],
                device_id=device,
                device_id_type=MESH,
            ).start()
            return carry

        lax.fori_loop(1, n, body, 0)

    def fan_wait(n, peer, target, me, recv):
        def body(o, carry):
            there, device = peer(o)
            pltpu.make_async_remote_copy(
                src_ref=target.at[there],
                dst_ref=target.at[there],
                send_sem=recv.at[there],
                recv_sem=recv.at[there],
                device_id=device,
                device_id_type=MESH,
            ).wait_recv()
            return carry

        lax.fori_loop(1, n, body, 0)

    def fan_drain(n, peer, source, send):
        def body(o, carry):
            there, device = peer(o)
            pltpu.make_async_remote_copy(
                src_ref=source(there),
                dst_ref=source(there),
                send_sem=send.at[there],
                recv_sem=send.at[there],
                device_id=device,
                device_id_type=MESH,
            ).wait_send()
            return carry

        lax.fori_loop(1, n, body, 0)

    load_hidden = pltpu.make_async_copy(hidden, hv, local_sem.at[0])
    load_attn = pltpu.make_async_copy(attn, av, local_sem.at[1])
    load_hidden.start()
    load_attn.start()

    barrier = pltpu.get_barrier_semaphore()

    def greet(n, peer):
        def body(o, carry):
            _, device = peer(o)
            pl.semaphore_signal(barrier, inc=1, device_id=device, device_id_type=MESH)
            return carry

        lax.fori_loop(1, n, body, 0)

    greet(nq, plane_peer)
    greet(nl, line_peer)

    odd16 = lax.rem(iota((16, 1), 0), 2) == 1

    def by_row(even, odd):
        return jnp.where(odd16, odd, even)

    def pair_sum(x):
        even = jnp.sum(jnp.where(odd16, 0.0, x), axis=0, keepdims=True)
        odd = jnp.sum(jnp.where(odd16, x, 0.0), axis=0, keepdims=True)
        return by_row(even, odd)

    def chunk(k):
        return slice(k * wc, (k + 1) * wc)

    for k in range(8):
        unit_s[2 * k : 2 * k + 2, :] = queries[:, chunk(k)].astype(F32)
    query16 = unit_s[...]
    qnorm = jnp.sqrt(pair_sum(jnp.sum(query16 * query16, axis=1, keepdims=True)) + 1e-06)
    unit16 = query16 / qnorm
    unit_s[...] = unit16
    ub[l_me, :, 0:wc] = unit16.astype(BF16)
    place = jnp.broadcast_to(by_row(positives[0], positives[1]), (16, 128))
    lane16 = iota((16, 128), 1)
    high_place = lax.shift_right_logical(place, 4)
    digits = jnp.where(lane16 == 0, high_place, jnp.where(lane16 == 1, place - 16 * high_place, 0))
    ub[l_me, :, wc:] = digits.astype(F32).astype(BF16)

    pl.semaphore_wait(barrier, nq - 1 + nl - 1)
    fan_out(nl, line_peer, lambda there: ub.at[l_me], ub, l_me, u_send, u_recv)

    load_hidden.wait()

    def squares(i, carry):
        rows = pl.ds(pl.multiple_of(i * 16, 16), 16)
        v = hv[rows, :].astype(F32)
        ssq_s[rows, :] = jnp.broadcast_to(jnp.sum(v * v, axis=1, keepdims=True), (16, 128))
        return carry

    lax.fori_loop(0, tok // 16, squares, 0)
    ssq_row = jnp.transpose(ssq_s[...])[0:1, :]
    rstd = lax.rsqrt(ssq_row * (1.0 / width) + 1e-05)
    token = iota((1, tok), 1)
    inside0 = (token >= offsets[0]) & (token < offsets[0] + lengths[0])
    inside1 = (token >= offsets[1]) & (token < offsets[1] + lengths[1])
    w0 = jnp.where(inside0, rstd, 0.0)
    w1 = jnp.where(inside1, rstd, 0.0)
    counts = by_row(lengths[0].astype(F32), lengths[1].astype(F32))
    row16 = iota((16, 1), 0)
    wh, wm, wl = split3(jnp.where(odd16, w1, w0))
    part = lax.div(row16, 2)
    w3 = jnp.where(part == 0, wh, jnp.where(part == 1, wm, jnp.where(part == 2, wl, 0.0))).astype(BF16)
    for k in range(8):
        p = mm(w3, hv[:, chunk(k)])
        pool_s[2 * k : 2 * k + 2, :] = (p[0:2] + p[2:4] + p[4:6]) * gain[0:1, chunk(k)]
    pooled = pool_s[...] / counts
    pnorm = jnp.sqrt(pair_sum(jnp.sum(pooled * pooled, axis=1, keepdims=True)) + 1e-06)
    embed = pooled / pnorm
    eb[q_me] = embed.astype(BF16)
    fan_out(nq, plane_peer, lambda there: eb.at[q_me], eb, q_me, e_send, e_recv)

    load_attn.wait()
    flt = mm(down_t[...], av[...], NT).astype(BF16)
    hut = mm(up[...], hv[...], NT)
    na, nb = 16 * nq, 16 * nl
    np_, nqr = 2 * nq, 2 * nl

    def spread(rows, cols, row_is_block):
        small = iota((rows, cols), 0 if row_is_block else 1)
        big = iota((rows, cols), 1 if row_is_block else 0)
        return small == 2 * lax.div(big, 16) + lax.rem(big, 2)

    def as_f32(m):
        return jnp.where(m, 1.0, 0.0)

    same_chunk = lax.div(lax.rem(iota((na, nb), 0), 16), 2) == lax.div(lax.rem(iota((na, nb), 1), 16), 2)
    gather_a = as_f32(spread(np_, na, True))
    gather_b = as_f32(spread(nb, 128, False))
    first_b = as_f32(spread(nb, 128, False) & (lax.rem(iota((nb, 128), 0), 16) < 2))
    scatter_a = as_f32(spread(na, np_, False)).astype(BF16)
    scatter_b = as_f32(spread(128, nb, True)).astype(BF16)

    fan_wait(nl, line_peer, ub, l_me, u_recv)
    ubm = ub[:, :, 0:wc].reshape(nb, wc)
    digit = as_f32(iota((16, 128), 0) == iota((16, 128), 1)).astype(BF16)
    place_b = mm(digit, ub[:, :, wc:].reshape(nb, 128), NT).astype(BF16)
    place_i = mm(place_b, first_b.astype(BF16))
    pos = 16.0 * place_i[0:1, :] + place_i[1:2, :]
    passage = iota((np_, 1), 0)
    number = 2 * (grp * 2 * nq + 2 * lax.div(passage, 2) + core) + lax.rem(passage, 2)
    used = iota((1, 128), 1) < nqr
    target = jnp.where((number.astype(F32) == pos) & used, 1.0, 0.0)

    fan_wait(nq, plane_peer, eb, q_me, e_recv)
    ebm = eb[...].reshape(na, wc)
    products = jnp.where(same_chunk, mm(ebm, ubm, NT), 0.0)
    logits = 50.0 * mm(mm(gather_a, products, precision=HI), gather_b, precision=HI)
    expo = jnp.where(used, jnp.exp(logits), 0.0)
    partial = jnp.sum(expo, axis=0, keepdims=True)
    chosen = jnp.sum(logits * target, axis=0, keepdims=True)
    row8 = iota((8, 128), 0)
    lx[l_me] = jnp.where(row8 == 0, partial, jnp.where(row8 == 1, chosen, 0.0))
    fan_out(nl, line_peer, lambda there: lx.at[l_me], lx, l_me, x_send, x_recv)
    fan_wait(nl, line_peer, lx, l_me, x_recv)
    line = jnp.sum(lx[...], axis=0)
    lse = jnp.log(jnp.where(used, line[0:1, :], 1.0))
    line_loss = jnp.sum(jnp.where(used, lse - line[1:2, :], 0.0), axis=1, keepdims=True)
    prob = jnp.exp(logits - lse)
    grad = jnp.where(used, (prob - target) * 1024.0, 0.0).astype(BF16)
    spread_grad = mm(mm(scatter_a, grad).astype(BF16), scatter_b)
    g1 = jnp.where(same_chunk, spread_grad, 0.0)
    dpb[:, :, 0:wc] = mm(g1.astype(BF16), ubm).reshape(nq, 16, wc)
    dpb[:, :, wc:] = jnp.broadcast_to(jnp.where(iota((1, 1, 128), 2) == q_me, line_loss.reshape(1, 1, 1), 0.0), (nq, 16, 128))
    rb[q_me] = dpb[q_me]
    fan_out(nq, plane_peer, lambda there: dpb.at[there], rb, q_me, d_send, d_recv)
    dub[...] = mm(jnp.transpose(g1).astype(BF16), ebm).reshape(nl, 16, wc)
    rub[l_me] = dub[l_me]
    fan_out(nl, line_peer, lambda there: dub.at[there], rub, l_me, v_send, v_recv)

    fan_wait(nq, plane_peer, rb, q_me, d_recv)
    gathered = jnp.sum(rb[...], axis=0)
    loss_out[...] = jnp.broadcast_to(
        jnp.sum(gathered[0:8, wc:], axis=1, keepdims=True) * (1.0 / passages), (8, 128)
    )
    d_embed = 50.0 * gathered[:, 0:wc]
    along = pair_sum(jnp.sum(embed * d_embed, axis=1, keepdims=True))
    pool_s[...] = (d_embed - embed * along) / pnorm / counts
    dn_s[...] = jnp.zeros_like(dn_s)
    for k in range(8):
        dn = pool_s[2 * k : 2 * k + 2, :] * gain[0:1, chunk(k)]
        dh, dm, dl = split3(dn)
        dn_s[0:2, chunk(k)] = dh
        dn_s[2:4, chunk(k)] = dm
        dn_s[4:6, chunk(k)] = dl
        dn_s[8:10, chunk(k)] = dn
    dn3 = jnp.where(row16 < 6, dn_s[...], 0.0).astype(BF16)

    s3 = mm(dn3, hv[...], NT)
    s0 = s3[0:1] + s3[2:3] + s3[4:5]
    s1 = s3[1:2] + s3[3:4] + s3[5:6]
    s = jnp.where(inside0, s0, jnp.where(inside1, s1, 0.0))
    b = rstd * rstd * rstd * s * (1.0 / width)
    u3 = mm(up[...], dn3, NT)
    u0 = u3[:, 0:1] + u3[:, 2:3] + u3[:, 4:5]
    u1 = u3[:, 1:2] + u3[:, 3:4] + u3[:, 5:6]
    blt = (2.0 * (u0 * w0 + u1 * w1 - b * hut)).astype(BF16)
    blt_out[...] = blt
    tiles_down, tiles_up = feat // 128, width // 128
    per = (tiles_down + tiles_up) // nq

    def put(t, x):
        ab[t // per, :, (t % per) * 128 : (t % per) * 128 + 128] = x

    def get(ref, t):
        return ref[t // per, :, (t % per) * 128 : (t % per) * 128 + 128]

    down_part = mm(blt, av[...])
    for t in range(tiles_down):
        put(t, down_part[:, t * 128 : t * 128 + 128])
    fl = flt.astype(F32)
    fb = b * fl
    fbh = fb.astype(BF16)
    fbl = (fb - fbh.astype(F32)).astype(BF16)
    f0 = jnp.sum(w0 * fl, axis=1, keepdims=True)
    f1 = jnp.sum(w1 * fl, axis=1, keepdims=True)
    for k in range(8):
        hk = hv[:, chunk(k)]
        up2 = mm(fbh, hk) + mm(fbl, hk)
        up_part = 2.0 * (f0 * dn_s[8:9, chunk(k)] + f1 * dn_s[9:10, chunk(k)] - up2)
        for t in range(wc // 128):
            put(tiles_down + k * (wc // 128) + t, up_part[:, t * 128 : t * 128 + 128])

    def half(which):
        return pl.ds(pl.multiple_of(8 * which, 8), 8)

    other = 1 - core
    swap = pltpu.make_async_remote_copy(
        src_ref=ab.at[:, half(other), :],
        dst_ref=core_in,
        send_sem=c_send,
        recv_sem=c_recv,
        device_id=(grp, 2 * q_me + other),
        device_id_type=MESH,
    )
    swap.start()

    cols = jnp.where(
        iota((128, tok), 0) == 0, w0, jnp.where(iota((128, tok), 0) == 1, w1, b)
    )
    col_s[...] = jnp.transpose(cols)
    swap.wait()
    mine = half(core)
    core_in[...] = core_in[...] + ab[:, mine, :]
    plane_in[q_me] = core_in[q_me]
    fan_out(nq, plane_peer, lambda there: core_in.at[there], plane_in, q_me, p_send, p_recv)

    def rows_dy(i, carry):
        rows = pl.ds(pl.multiple_of(i * 16, 16), 16)
        c = col_s[rows, :]
        v = hv[rows, :].astype(F32)
        dyv[rows, :] = (c[:, 0:1] * dn_s[8:9, :] + c[:, 1:2] * dn_s[9:10, :] - c[:, 2:3] * v).astype(BF16)
        return carry

    lax.fori_loop(0, tok // 16, rows_dy, 0)
    store_dy = pltpu.make_async_copy(dyv, dy_out, local_sem.at[2])
    store_dy.start()

    fan_wait(nq, plane_peer, plane_in, q_me, p_recv)
    z_in[grp] = jnp.sum(plane_in[...], axis=0)
    fan_out(ng, z_peer, lambda there: z_in.at[grp], z_in, grp, z_send, z_recv)

    fan_wait(nl, line_peer, rub, l_me, v_recv)
    d_unit = 50.0 * jnp.sum(rub[...], axis=0)
    unit = unit_s[...]
    unit_s[...] = (d_unit - unit * pair_sum(jnp.sum(unit * d_unit, axis=1, keepdims=True))) / qnorm
    for k in range(8):
        query_out[:, chunk(k)] = unit_s[2 * k : 2 * k + 2, :]

    fan_wait(ng, z_peer, z_in, grp, z_recv)
    total_s[q_me, mine, :] = jnp.sum(z_in[...], axis=0)

    def gather_piece(o, carry):
        there, device = plane_peer(o)
        pltpu.make_async_remote_copy(
            src_ref=total_s.at[q_me, mine, :],
            dst_ref=total_s.at[q_me, mine, :],
            send_sem=g_send.at[there],
            recv_sem=g_recv.at[q_me],
            device_id=device,
            device_id_type=MESH,
        ).start()
        return carry

    def gather_wait(o, carry):
        there, device = plane_peer(o)
        piece = total_s.at[there, mine, :]
        pltpu.make_async_remote_copy(
            src_ref=piece,
            dst_ref=piece,
            send_sem=g_send.at[there],
            recv_sem=g_recv.at[there],
            device_id=device,
            device_id_type=MESH,
        ).wait()
        return carry

    lax.fori_loop(1, nq, gather_piece, 0)
    lax.fori_loop(1, nq, gather_wait, 0)
    back = pltpu.make_async_remote_copy(
        src_ref=total_s.at[:, mine, :],
        dst_ref=total_s.at[:, mine, :],
        send_sem=s_send,
        recv_sem=s_recv,
        device_id=(grp, 2 * q_me + other),
        device_id_type=MESH,
    )
    back.start()
    fan_drain(nl, line_peer, lambda there: ub.at[there], u_send)
    fan_drain(nq, plane_peer, lambda there: eb.at[there], e_send)
    fan_drain(nl, line_peer, lambda there: lx.at[there], x_send)
    fan_drain(nq, plane_peer, lambda there: dpb.at[there], d_send)
    fan_drain(nl, line_peer, lambda there: dub.at[there], v_send)
    fan_drain(nq, plane_peer, lambda there: core_in.at[there], p_send)
    fan_drain(ng, z_peer, lambda there: z_in.at[there], z_send)
    store_dy.wait()
    back.wait()
    for t in range(tiles_down + tiles_up):
        adapter_out[:, t * 128 : t * 128 + 128] = get(total_s, t)


def per_device(ng, nq, attn, hidden, weight, down, up, gain, queries, lengths, offsets, positives):
    tok, width = hidden.shape
    feat = attn.shape[1]
    wc = width // 8
    nl = 2 * ng
    piece = (feat + width) // nq
    down_t = down.T
    vmem = pl.BlockSpec(memory_space=pltpu.VMEM)
    smem = pl.BlockSpec(memory_space=pltpu.SMEM)
    anywhere = pl.BlockSpec(memory_space=pl.ANY)
    dma = pltpu.SemaphoreType.DMA
    everything = lax.all_gather(weight, "dp", axis=0, tiled=True)
    dy, blt, query_gradient, adapters, loss = pl.pallas_call(
        functools.partial(kernel, ng, nq),
        out_shape=(
            jax.ShapeDtypeStruct((tok, width), BF16),
            jax.ShapeDtypeStruct((16, tok), BF16),
            jax.ShapeDtypeStruct((2, width), F32),
            jax.ShapeDtypeStruct((16, feat + width), F32),
            jax.ShapeDtypeStruct((8, 128), F32),
        ),
        in_specs=[anywhere, anywhere, vmem, vmem, vmem, vmem, smem, smem, smem],
        out_specs=(anywhere, vmem, vmem, vmem, vmem),
        scratch_shapes=[
            pltpu.VMEM((tok, width), BF16),
            pltpu.VMEM((tok, feat), BF16),
            pltpu.VMEM((tok, width), BF16),
            pltpu.VMEM((nl, 16, wc + 128), BF16),
            pltpu.VMEM((nq, 16, wc), BF16),
            pltpu.VMEM((16, wc), F32),
            pltpu.VMEM((16, wc), F32),
            pltpu.VMEM((tok, 128), F32),
            pltpu.VMEM((tok, 128), F32),
            pltpu.VMEM((16, width), F32),
            pltpu.VMEM((nl, 8, 128), F32),
            pltpu.VMEM((nq, 16, wc + 128), F32),
            pltpu.VMEM((nq, 16, wc + 128), F32),
            pltpu.VMEM((nl, 16, wc), F32),
            pltpu.VMEM((nl, 16, wc), F32),
            pltpu.VMEM((nq, 16, piece), F32),
            pltpu.VMEM((nq, 8, piece), F32),
            pltpu.VMEM((nq, 8, piece), F32),
            pltpu.VMEM((ng, 8, piece), F32),
            pltpu.VMEM((nq, 16, piece), F32),
            dma((3,)),
            dma((nl,)),
            dma((nl,)),
            dma((nq,)),
            dma((nq,)),
            dma((nl,)),
            dma((nl,)),
            dma((nq,)),
            dma((nq,)),
            dma((nl,)),
            dma((nl,)),
            dma,
            dma,
            dma((nq,)),
            dma((nq,)),
            dma((ng,)),
            dma((ng,)),
            dma((nq,)),
            dma((nq,)),
            dma,
            dma,
        ],
        compiler_params=pltpu.CompilerParams(
            collective_id=0, has_side_effects=True, vmem_limit_bytes=40 * 1024 * 1024
        ),
    )(hidden, attn, down_t, up, gain.reshape(1, width), queries, lengths, offsets, positives)
    attention_gradient = (
        mm(dy, everything, NT) + mm(blt, down_t, TN)
    ).astype(BF16)
    return (
        attention_gradient,
        query_gradient,
        adapters[:, 0:feat].T,
        adapters[:, feat:],
        loss[0, 0],
    )


def solution(mesh):
    ng = mesh.shape["grp"]
    nq = mesh.shape["dp"] // 2
    both = P(("grp", "dp"))
    rows = P(("grp", "dp"), None)
    return jax.shard_map(
        functools.partial(per_device, ng, nq),
        mesh=mesh,
        in_specs=(rows, rows, P("dp", None), P(), P(), P(), rows, both, both, both),
        out_specs=(rows, rows, P(), P(), P()),
        check_vma=False,
    )
```

```python
import functools

import jax
import jax.numpy as jnp
from jax import lax
from jax.experimental import pallas as pl
from jax.experimental.pallas import tpu as pltpu
from jax.sharding import PartitionSpec as P

MESH = pl.DeviceIdType.MESH
F32 = jnp.float32
BF16 = jnp.bfloat16
HI = lax.Precision.HIGHEST
CUT = 3072
NT = (((1,), (1,)), ((), ()))
TN = (((0,), (0,)), ((), ()))


def iota(shape, dim):
    return lax.broadcasted_iota(jnp.int32, shape, dim)


def mm(a, b, dims=None, precision=None):
    if dims is None:
        dims = (((1,), (0,)), ((), ()))
    return lax.dot_general(a, b, dims, precision=precision, preferred_element_type=F32)


def split3(x):
    high = x.astype(BF16).astype(F32)
    rest = x - high
    mid = rest.astype(BF16).astype(F32)
    return high, mid, (rest - mid).astype(BF16).astype(F32)


def kernel(
    ng,
    nq,
    hidden,
    attn,
    weight,
    down_h,
    up_h,
    gain_h,
    queries_h,
    lengths_h,
    offsets_h,
    positives_h,
    attn_out,
    query_out,
    down_out,
    up_out,
    loss_out,
    hv,
    av,
    wv,
    dyv,
    ov,
    down_t,
    up,
    gain,
    queries,
    lengths,
    offsets,
    positives,
    ub,
    eb,
    unit_s,
    pool_s,
    ssq_s,
    col_s,
    bl_s,
    dn_s,
    lx,
    dpb,
    rb,
    dub,
    rub,
    ab,
    core_in,
    plane_in,
    z_in,
    total_s,
    query_s,
    loss_s,
    sum_s,
    local_sem,
    out_sem,
    u_send,
    u_recv,
    e_send,
    e_recv,
    x_send,
    x_recv,
    d_send,
    d_recv,
    v_send,
    v_recv,
    c_send,
    c_recv,
    p_send,
    p_recv,
    z_send,
    z_recv,
    g_send,
    g_recv,
    s_send,
    s_recv,
    w_send,
    w_recv,
    wz_send,
    wz_recv,
    wc_send,
    wc_recv,
):
    nl = 2 * ng
    tok, width = hv.shape
    wc = width // 8
    feat = av.shape[1]
    passages = 2 * nl * nq
    grp = lax.axis_index("grp")
    dp = lax.axis_index("dp")
    core = lax.rem(dp, 2)
    q_me = lax.div(dp, 2)
    l_me = 2 * grp + core

    def plane_peer(o):
        q = lax.rem(q_me + o, nq)
        return q, (grp, 2 * q + core)

    def line_peer(o):
        l = lax.rem(l_me + o, nl)
        return l, (lax.div(l, 2), 2 * q_me + lax.rem(l, 2))

    def z_peer(o):
        z = lax.rem(grp + o, ng)
        return z, (z, dp)

    def fan_out(n, peer, source, target, me, send, recv):
        def body(o, carry):
            there, device = peer(o)
            pltpu.make_async_remote_copy(
                src_ref=source(there),
                dst_ref=target.at[me],
                send_sem=send.at[there],
                recv_sem=recv.at[me],
                device_id=device,
                device_id_type=MESH,
            ).start()
            return carry

        lax.fori_loop(1, n, body, 0)

    def fan_wait(n, peer, target, me, recv):
        def body(o, carry):
            there, device = peer(o)
            pltpu.make_async_remote_copy(
                src_ref=target.at[there],
                dst_ref=target.at[there],
                send_sem=recv.at[there],
                recv_sem=recv.at[there],
                device_id=device,
                device_id_type=MESH,
            ).wait_recv()
            return carry

        lax.fori_loop(1, n, body, 0)

    def fan_drain(n, peer, source, send):
        def body(o, carry):
            there, device = peer(o)
            pltpu.make_async_remote_copy(
                src_ref=source(there),
                dst_ref=source(there),
                send_sem=send.at[there],
                recv_sem=send.at[there],
                device_id=device,
                device_id_type=MESH,
            ).wait_send()
            return carry

        lax.fori_loop(1, n, body, 0)

    def load(source, target, i):
        copy = pltpu.make_async_copy(source, target, local_sem.at[i])
        copy.start()
        return copy

    load_queries = load(queries_h, queries, 0)
    load_positives = load(positives_h, positives, 1)
    load_hidden = load(hidden, hv, 2)
    load_weight = load(weight, wv.at[dp], 3)
    load_rest = [
        load(gain_h, gain, 4),
        load(lengths_h, lengths, 5),
        load(offsets_h, offsets, 6),
    ]
    load_attn = load(attn, av, 7)
    load_down = load(down_h, down_t, 8)
    load_up = load(up_h, up, 9)

    barrier = pltpu.get_barrier_semaphore()

    def greet(n, peer):
        def body(o, carry):
            _, device = peer(o)
            pl.semaphore_signal(barrier, inc=1, device_id=device, device_id_type=MESH)
            return carry

        lax.fori_loop(1, n, body, 0)

    greet(nq, plane_peer)
    greet(nl, line_peer)

    x_me = lax.rem(q_me, 4)
    y_me = lax.div(q_me, 4)
    parity = lax.rem(grp, 2)

    def along(axis, o):
        if axis == 0:
            return 4 * y_me + lax.rem(x_me + o, 4)
        return 4 * lax.rem(y_me + o, 4) + x_me

    def w_rows(whose, part):
        return pl.ds(pl.multiple_of(32 * whose + 16 * part, 16), 16)

    def w_pieces(q, part):
        d = 2 * q + core
        pieces = [wv.at[d, w_rows(parity, part), :]]
        if CUT < width:
            pieces.append(wv.at[d, w_rows(1 - parity, part), CUT:])
        return pieces

    def w_copy(q, part, to, a, b):
        for r, piece in enumerate(w_pieces(q, part)):
            pltpu.make_async_remote_copy(
                src_ref=piece,
                dst_ref=piece,
                send_sem=w_send.at[r, part, a, b],
                recv_sem=w_recv.at[r, part, q],
                device_id=(grp, 2 * to + core),
                device_id_type=MESH,
            ).start()

    def w_wait(q, part):
        for r, piece in enumerate(w_pieces(q, part)):
            pltpu.make_async_remote_copy(
                src_ref=piece,
                dst_ref=piece,
                send_sem=w_recv.at[r, part, q],
                recv_sem=w_recv.at[r, part, q],
                device_id=(grp, dp),
                device_id_type=MESH,
            ).wait_recv()

    def w_own(part, b):
        w_copy(q_me, part, along(part, b), 4, b)

    def w_relay(part, a, b):
        w_copy(along(part, a), part, along(1 - part, b), a, b)

    def z_copies(q):
        d = 2 * q + core
        for part, o in ((0, ng - 1), (1, 1)):
            piece = wv.at[d, w_rows(parity, part), 0:CUT]
            yield pltpu.make_async_remote_copy(
                src_ref=piece,
                dst_ref=piece,
                send_sem=wz_send.at[part, q],
                recv_sem=wz_recv.at[part, q],
                device_id=(lax.rem(grp + o, ng), dp),
                device_id_type=MESH,
            )

    def w_across(q):
        for copy in z_copies(q):
            copy.start()

    def w_across_wait(q):
        d = 2 * q + core
        for part in (0, 1):
            piece = wv.at[d, w_rows(1 - parity, part), 0:CUT]
            pltpu.make_async_remote_copy(
                src_ref=piece,
                dst_ref=piece,
                send_sem=wz_recv.at[part, q],
                recv_sem=wz_recv.at[part, q],
                device_id=(grp, dp),
                device_id_type=MESH,
            ).wait_recv()

    def core_copy(q, side):
        chunk_ref = wv.at[2 * q + side]
        return pltpu.make_async_remote_copy(
            src_ref=chunk_ref,
            dst_ref=chunk_ref,
            send_sem=wc_send.at[q],
            recv_sem=wc_recv.at[q],
            device_id=(grp, 2 * q_me + 1 - core),
            device_id_type=MESH,
        )

    def at(oy, ox):
        return 4 * lax.rem(y_me + oy, 4) + lax.rem(x_me + ox, 4)

    def w_step0():
        load_weight.wait()
        for b in (1, 3):
            for part in (0, 1):
                w_own(part, b)
                w_relay(part, 0, b)
        core_copy(q_me, core).start()

    def w_step1():
        for part in (0, 1):
            w_own(part, 2)
            w_relay(part, 0, 2)

    def w_step2():
        for part in (0, 1):
            for a in (1, 3):
                w_wait(along(part, a), part)
        for a in (1, 3):
            for b in (1, 3):
                for part in (0, 1):
                    w_relay(part, a, b)
        for part in (0, 1):
            for a in (1, 3):
                w_wait(along(part, a), 1 - part)
                w_across(along(part, a))

    def w_step3():
        for a in (1, 3):
            for part in (0, 1):
                w_relay(part, a, 2)

    def w_step4():
        for part in (0, 1):
            w_wait(along(part, 2), part)
        for b in (1, 2, 3):
            for part in (0, 1):
                w_relay(part, 2, b)

    def w_step5():
        for part in (0, 1):
            w_wait(along(part, 2), 1 - part)
            w_across(along(part, 2))
        for oy in (1, 3):
            for ox in (1, 3):
                w_wait(at(oy, ox), 0)
                w_wait(at(oy, ox), 1)
                w_across(at(oy, ox))

    def w_step6():
        for oy, ox in ((1, 2), (3, 2), (2, 1), (2, 3), (2, 2)):
            w_wait(at(oy, ox), 0)
            w_wait(at(oy, ox), 1)
            w_across(at(oy, ox))

    def tile_at(t):
        k = lax.div(t, 2)
        oy = jnp.where(k == 2, 3, jnp.where(k == 3, 2, k))
        near = lax.div(x_me, 2)
        pair = lax.rem(near + lax.rem(t, 2), 2)
        return 2 * lax.rem(y_me + oy, 4) + pair

    def w_finish(q):
        w_across_wait(q)
        core_copy(q, core).start()

    def tile_start(t):
        n = tile_at(t)
        w_finish(2 * n)
        w_finish(2 * n + 1)

    def tile(t, carry):
        n = tile_at(t)
        core_copy(2 * n, 1 - core).wait_recv()
        core_copy(2 * n + 1, 1 - core).wait_recv()
        columns = pl.ds(pl.multiple_of(256 * n, 256), 256)
        w_tile = wv[pl.ds(4 * n, 4)].reshape(256, width)
        out = mm(dyv[...], w_tile, NT) + mm(bl_s[:, 0:16], down_t[:, columns])
        ov[:, columns] = out.astype(BF16)
        pltpu.make_async_copy(ov.at[:, columns], attn_out.at[:, columns], out_sem.at[t]).start()
        return carry

    def tile_stored(t, carry):
        columns = pl.ds(pl.multiple_of(256 * tile_at(t), 256), 256)
        pltpu.make_async_copy(ov.at[:, columns], attn_out.at[:, columns], out_sem.at[t]).wait()
        return carry

    def w_drain():
        for part in (0, 1):
            for b in (1, 2, 3):
                for a in (0, 1, 2, 3, 4):
                    q = q_me if a == 4 else along(part, a)
                    for r, piece in enumerate(w_pieces(q, part)):
                        pltpu.make_async_remote_copy(
                            src_ref=piece,
                            dst_ref=piece,
                            send_sem=w_send.at[r, part, a, b],
                            recv_sem=w_send.at[r, part, a, b],
                            device_id=(grp, dp),
                            device_id_type=MESH,
                        ).wait_send()

        def body(o, carry):
            q = lax.rem(q_me + o, nq)
            for copy in z_copies(q):
                copy.wait_send()
            core_copy(q, core).wait_send()
            return carry

        lax.fori_loop(1, nq, body, 0)
        core_copy(q_me, core).wait_send()

    odd16 = lax.rem(iota((16, 1), 0), 2) == 1

    def by_row(even, odd):
        return jnp.where(odd16, odd, even)

    def pair_sum(x):
        even = jnp.sum(jnp.where(odd16, 0.0, x), axis=0, keepdims=True)
        odd = jnp.sum(jnp.where(odd16, x, 0.0), axis=0, keepdims=True)
        return by_row(even, odd)

    def chunk(k):
        return slice(k * wc, (k + 1) * wc)

    load_queries.wait()
    load_positives.wait()
    for k in range(8):
        unit_s[2 * k : 2 * k + 2, :] = queries[:, chunk(k)].astype(F32)
    query16 = unit_s[...]
    qnorm = jnp.sqrt(pair_sum(jnp.sum(query16 * query16, axis=1, keepdims=True)) + 1e-06)
    unit16 = query16 / qnorm
    unit_s[...] = unit16
    ub[l_me, :, 0:wc] = unit16.astype(BF16)
    place = jnp.broadcast_to(by_row(positives[0], positives[1]), (16, 128))
    lane16 = iota((16, 128), 1)
    high_place = lax.shift_right_logical(place, 4)
    digits = jnp.where(lane16 == 0, high_place, jnp.where(lane16 == 1, place - 16 * high_place, 0))
    ub[l_me, :, wc:] = digits.astype(F32).astype(BF16)

    pl.semaphore_wait(barrier, nq - 1 + nl - 1)
    fan_out(nl, line_peer, lambda there: ub.at[l_me], ub, l_me, u_send, u_recv)
    w_step0()

    load_hidden.wait()

    def squares(i, carry):
        rows = pl.ds(pl.multiple_of(i * 16, 16), 16)
        v = hv[rows, :].astype(F32)
        v = v * v
        total = v[:, 0:128]
        for t in range(1, width // 128):
            total = total + v[:, t * 128 : t * 128 + 128]
        ssq_s[rows, :] = total
        return carry

    lax.fori_loop(0, tok // 16, squares, 0, unroll=2)
    ssq_row = mm(jnp.ones((8, 128), F32), ssq_s[...], NT, HI)[0:1, :]
    for copy in load_rest:
        copy.wait()
    rstd = lax.rsqrt(ssq_row * (1.0 / width) + 1e-05)
    token = iota((1, tok), 1)
    inside0 = (token >= offsets[0]) & (token < offsets[0] + lengths[0])
    inside1 = (token >= offsets[1]) & (token < offsets[1] + lengths[1])
    w0 = jnp.where(inside0, rstd, 0.0)
    w1 = jnp.where(inside1, rstd, 0.0)
    counts = by_row(lengths[0].astype(F32), lengths[1].astype(F32))
    row16 = iota((16, 1), 0)
    wh, wm, wl = split3(jnp.where(odd16, w1, w0))
    part = lax.div(row16, 2)
    w3 = jnp.where(part == 0, wh, jnp.where(part == 1, wm, jnp.where(part == 2, wl, 0.0))).astype(BF16)
    for k in range(8):
        p = mm(w3, hv[:, chunk(k)])
        pool_s[2 * k : 2 * k + 2, :] = (p[0:2] + p[2:4] + p[4:6]) * gain[0:1, chunk(k)]
    pooled = pool_s[...] / counts
    pnorm = jnp.sqrt(pair_sum(jnp.sum(pooled * pooled, axis=1, keepdims=True)) + 1e-06)
    embed = pooled / pnorm
    eb[q_me] = embed.astype(BF16)
    fan_out(nq, plane_peer, lambda there: eb.at[q_me], eb, q_me, e_send, e_recv)
    w_step1()

    load_attn.wait()
    load_down.wait()
    load_up.wait()
    flt = mm(down_t[...], av[...], NT).astype(BF16)
    hut = mm(up[...], hv[...], NT)
    na, nb = 16 * nq, 16 * nl
    np_, nqr = 2 * nq, 2 * nl

    def spread(rows, cols, row_is_block):
        small = iota((rows, cols), 0 if row_is_block else 1)
        big = iota((rows, cols), 1 if row_is_block else 0)
        return small == 2 * lax.div(big, 16) + lax.rem(big, 2)

    def as_f32(m):
        return jnp.where(m, 1.0, 0.0)

    same_chunk = lax.div(lax.rem(iota((na, nb), 0), 16), 2) == lax.div(lax.rem(iota((na, nb), 1), 16), 2)
    gather_a = as_f32(spread(np_, na, True))
    gather_b = as_f32(spread(nb, 128, False))
    first_b = as_f32(spread(nb, 128, False) & (lax.rem(iota((nb, 128), 0), 16) < 2))
    scatter_a = as_f32(spread(na, np_, False)).astype(BF16)
    scatter_b = as_f32(spread(128, nb, True)).astype(BF16)

    fan_wait(nl, line_peer, ub, l_me, u_recv)
    ubm = ub[:, :, 0:wc].reshape(nb, wc)
    digit = as_f32(iota((16, 128), 0) == iota((16, 128), 1)).astype(BF16)
    place_b = mm(digit, ub[:, :, wc:].reshape(nb, 128), NT).astype(BF16)
    place_i = mm(place_b, first_b.astype(BF16))
    pos = 16.0 * place_i[0:1, :] + place_i[1:2, :]
    passage = iota((np_, 1), 0)
    number = 2 * (grp * 2 * nq + 2 * lax.div(passage, 2) + core) + lax.rem(passage, 2)
    used = iota((1, 128), 1) < nqr
    target = jnp.where((number.astype(F32) == pos) & used, 1.0, 0.0)

    fan_wait(nq, plane_peer, eb, q_me, e_recv)
    ebm = eb[...].reshape(na, wc)
    products = jnp.where(same_chunk, mm(ebm, ubm, NT), 0.0)
    logits = 50.0 * mm(mm(gather_a, products, precision=HI), gather_b, precision=HI)
    expo = jnp.where(used, jnp.exp(logits), 0.0)
    partial = jnp.sum(expo, axis=0, keepdims=True)
    chosen = jnp.sum(logits * target, axis=0, keepdims=True)
    row8 = iota((8, 128), 0)
    lx[l_me] = jnp.where(row8 == 0, partial, jnp.where(row8 == 1, chosen, 0.0))
    fan_out(nl, line_peer, lambda there: lx.at[l_me], lx, l_me, x_send, x_recv)
    w_step2()
    fan_wait(nl, line_peer, lx, l_me, x_recv)
    line = jnp.sum(lx[...], axis=0)
    lse = jnp.log(jnp.where(used, line[0:1, :], 1.0))
    line_loss = jnp.sum(jnp.where(used, lse - line[1:2, :], 0.0), axis=1, keepdims=True)
    prob = jnp.exp(logits - lse)
    grad = jnp.where(used, (prob - target) * 1024.0, 0.0).astype(BF16)
    spread_grad = mm(mm(scatter_a, grad).astype(BF16), scatter_b)
    g1 = jnp.where(same_chunk, spread_grad, 0.0)
    dpb[:, :, 0:wc] = mm(g1.astype(BF16), ubm).reshape(nq, 16, wc)
    dpb[:, :, wc:] = jnp.broadcast_to(jnp.where(iota((1, 1, 128), 2) == q_me, line_loss.reshape(1, 1, 1), 0.0), (nq, 16, 128))
    rb[q_me] = dpb[q_me]
    fan_out(nq, plane_peer, lambda there: dpb.at[there], rb, q_me, d_send, d_recv)
    w_step3()
    w_step4()
    dub[...] = mm(jnp.transpose(g1).astype(BF16), ebm).reshape(nl, 16, wc).astype(BF16)
    rub[l_me] = dub[l_me]
    fan_out(nl, line_peer, lambda there: dub.at[there], rub, l_me, v_send, v_recv)

    fan_wait(nq, plane_peer, rb, q_me, d_recv)
    gathered = jnp.sum(rb[...], axis=0)
    loss_s[...] = jnp.sum(gathered[0:1, wc:], axis=1, keepdims=True) * (1.0 / passages)
    d_embed = 50.0 * gathered[:, 0:wc]
    shared = pair_sum(jnp.sum(embed * d_embed, axis=1, keepdims=True))
    pool_s[...] = (d_embed - embed * shared) / pnorm / counts
    dn_s[...] = jnp.zeros_like(dn_s)
    for k in range(8):
        dn = pool_s[2 * k : 2 * k + 2, :] * gain[0:1, chunk(k)]
        dh, dm, dl = split3(dn)
        dn_s[0:2, chunk(k)] = dh
        dn_s[2:4, chunk(k)] = dm
        dn_s[4:6, chunk(k)] = dl
        dn_s[8:10, chunk(k)] = dn
    dn3 = jnp.where(row16 < 6, dn_s[...], 0.0).astype(BF16)

    s3 = mm(dn3, hv[...], NT)
    s0 = s3[0:1] + s3[2:3] + s3[4:5]
    s1 = s3[1:2] + s3[3:4] + s3[5:6]
    s = jnp.where(inside0, s0, jnp.where(inside1, s1, 0.0))
    b = rstd * rstd * rstd * s * (1.0 / width)
    u3 = mm(up[...], dn3, NT)
    u0 = u3[:, 0:1] + u3[:, 2:3] + u3[:, 4:5]
    u1 = u3[:, 1:2] + u3[:, 3:4] + u3[:, 5:6]
    blt = (2.0 * (u0 * w0 + u1 * w1 - b * hut)).astype(BF16)
    tiles_down, tiles_up = feat // 128, width // 128
    per = (tiles_down + tiles_up) // nq

    def put(t, x):
        ab[t // per, :, (t % per) * 128 : (t % per) * 128 + 128] = x

    def get(ref, t):
        return ref[t // per, :, (t % per) * 128 : (t % per) * 128 + 128]

    down_part = mm(blt, av[...])
    for t in range(tiles_down):
        put(t, down_part[:, t * 128 : t * 128 + 128])
    fl = flt.astype(F32)
    fb = b * fl
    fbh = fb.astype(BF16)
    fbl = (fb - fbh.astype(F32)).astype(BF16)
    f0 = jnp.sum(w0 * fl, axis=1, keepdims=True)
    f1 = jnp.sum(w1 * fl, axis=1, keepdims=True)
    fb2 = jnp.concatenate([fbh, fbl], axis=0)
    for k in range(8):
        up2 = mm(fb2, hv[:, chunk(k)])
        up2 = up2[0:16] + up2[16:32]
        up_part = 2.0 * (f0 * dn_s[8:9, chunk(k)] + f1 * dn_s[9:10, chunk(k)] - up2)
        for t in range(wc // 128):
            put(tiles_down + k * (wc // 128) + t, up_part[:, t * 128 : t * 128 + 128])

    def half(which):
        return pl.ds(pl.multiple_of(8 * which, 8), 8)

    other = 1 - core
    swap = pltpu.make_async_remote_copy(
        src_ref=ab.at[:, half(other), :],
        dst_ref=core_in,
        send_sem=c_send,
        recv_sem=c_recv,
        device_id=(grp, 2 * q_me + other),
        device_id_type=MESH,
    )
    swap.start()

    w_step5()
    swap.wait_recv()
    mine = half(core)
    core_in[...] = core_in[...] + ab[:, mine, :]
    plane_in[q_me] = core_in[q_me]
    fan_out(nq, plane_peer, lambda there: core_in.at[there], plane_in, q_me, p_send, p_recv)

    row_id = iota((128, tok), 0)
    col_s[...] = jnp.transpose(jnp.where(row_id == 0, w0 + w1, jnp.where(row_id == 1, b, 0.0)))
    blf = jnp.concatenate([blt.astype(F32), jnp.zeros((112, tok), F32)], axis=0)
    bl_s[...] = jnp.transpose(blf).astype(BF16)

    def rows_dy(i, carry):
        rows = pl.ds(pl.multiple_of(i * 16, 16), 16)
        c = col_s[rows, :]
        second = jnp.where(i * 16 >= offsets[1], 1, 0)
        dn_row = dn_s[pl.ds(8 + second, 1), :]
        dyv[rows, :] = (c[:, 0:1] * dn_row - c[:, 1:2] * hv[rows, :].astype(F32)).astype(BF16)
        return carry

    lax.fori_loop(0, tok // 16, rows_dy, 0, unroll=2)

    fan_wait(nq, plane_peer, plane_in, q_me, p_recv)
    z_in[grp] = jnp.sum(plane_in[...], axis=0)
    fan_out(ng, z_peer, lambda there: z_in.at[grp], z_in, grp, z_send, z_recv)
    w_step6()

    fan_wait(nl, line_peer, rub, l_me, v_recv)
    d_unit = 50.0 * jnp.sum(rub[...].astype(F32), axis=0)
    unit = unit_s[...]
    unit_s[...] = (d_unit - unit * pair_sum(jnp.sum(unit * d_unit, axis=1, keepdims=True))) / qnorm
    for k in range(8):
        query_s[:, chunk(k)] = unit_s[2 * k : 2 * k + 2, :]
    store_query = pltpu.make_async_copy(query_s, query_out, local_sem.at[10])
    store_query.start()
    store_loss = pltpu.make_async_copy(loss_s, loss_out, local_sem.at[11])
    store_loss.start()
    w_finish(4 * y_me + x_me + 1 - 2 * lax.rem(x_me, 2))
    tile_start(1)

    fan_wait(ng, z_peer, z_in, grp, z_recv)
    total_s[q_me, mine, :] = jnp.sum(z_in[...], axis=0)

    def gather_piece(o, carry):
        there, device = plane_peer(o)
        pltpu.make_async_remote_copy(
            src_ref=total_s.at[q_me, mine, :],
            dst_ref=total_s.at[q_me, mine, :],
            send_sem=g_send.at[there],
            recv_sem=g_recv.at[q_me],
            device_id=device,
            device_id_type=MESH,
        ).start()
        return carry

    def gather_wait(o, carry):
        there, device = plane_peer(o)
        piece = total_s.at[there, mine, :]
        pltpu.make_async_remote_copy(
            src_ref=piece,
            dst_ref=piece,
            send_sem=g_send.at[there],
            recv_sem=g_recv.at[there],
            device_id=device,
            device_id_type=MESH,
        ).wait_recv()
        return carry

    lax.fori_loop(1, nq, gather_piece, 0)
    tile(0, 0)
    tile_start(2)
    tile(1, 0)
    lax.fori_loop(1, nq, gather_wait, 0)
    back = pltpu.make_async_remote_copy(
        src_ref=total_s.at[:, mine, :],
        dst_ref=total_s.at[:, mine, :],
        send_sem=s_send,
        recv_sem=s_recv,
        device_id=(grp, 2 * q_me + other),
        device_id_type=MESH,
    )
    back.start()

    def tiles(t, carry):
        tile_start(t + 1)
        return tile(t, carry)

    lax.fori_loop(2, 7, tiles, 0)
    tile(7, 0)

    back.wait_recv()
    for t in range(tiles_down):
        sum_s[:, t * 128 : t * 128 + 128] = get(total_s, t)
    for t in range(tiles_up):
        sum_s[:, feat + t * 128 : feat + t * 128 + 128] = get(total_s, tiles_down + t)
    store_down = pltpu.make_async_copy(sum_s.at[:, 0:feat], down_out, local_sem.at[12])
    store_down.start()
    store_up = pltpu.make_async_copy(sum_s.at[:, feat:], up_out, local_sem.at[13])
    store_up.start()
    fan_drain(nl, line_peer, lambda there: ub.at[there], u_send)
    fan_drain(nq, plane_peer, lambda there: eb.at[there], e_send)
    fan_drain(nl, line_peer, lambda there: lx.at[there], x_send)
    fan_drain(nq, plane_peer, lambda there: dpb.at[there], d_send)
    fan_drain(nl, line_peer, lambda there: dub.at[there], v_send)
    fan_drain(nq, plane_peer, lambda there: core_in.at[there], p_send)
    fan_drain(ng, z_peer, lambda there: z_in.at[there], z_send)
    fan_drain(nq, plane_peer, lambda there: core_in.at[there], g_send)
    swap.wait_send()
    back.wait_send()
    w_drain()
    store_query.wait()
    store_loss.wait()
    store_down.wait()
    store_up.wait()
    lax.fori_loop(0, 8, tile_stored, 0)


def per_device(ng, nq, attn, hidden, weight, down, up, gain, queries, lengths, offsets, positives):
    tok, width = hidden.shape
    feat = attn.shape[1]
    wc = width // 8
    nl = 2 * ng
    piece = (feat + width) // nq
    hbm = pl.BlockSpec(memory_space=pltpu.HBM)
    dma = pltpu.SemaphoreType.DMA
    outs = (
        jax.ShapeDtypeStruct((tok, feat), BF16),
        jax.ShapeDtypeStruct((2, width), F32),
        jax.ShapeDtypeStruct((16, feat), F32),
        jax.ShapeDtypeStruct((16, width), F32),
        jax.ShapeDtypeStruct((1, 1), F32),
    )
    results = pl.pallas_call(
        functools.partial(kernel, ng, nq),
        out_shape=outs,
        in_specs=[hbm] * 10,
        out_specs=(hbm,) * 5,
        scratch_shapes=[
            pltpu.VMEM((tok, width), BF16),
            pltpu.VMEM((tok, feat), BF16),
            pltpu.VMEM((2 * nq, 64, width), BF16),
            pltpu.VMEM((tok, width), BF16),
            pltpu.VMEM((tok, feat), BF16),
            pltpu.VMEM((16, feat), BF16),
            pltpu.VMEM((16, width), BF16),
            pltpu.VMEM((1, width), F32),
            pltpu.VMEM((2, width), BF16),
            pltpu.SMEM((2,), jnp.int32),
            pltpu.SMEM((2,), jnp.int32),
            pltpu.SMEM((2,), jnp.int32),
            pltpu.VMEM((nl, 16, wc + 128), BF16),
            pltpu.VMEM((nq, 16, wc), BF16),
            pltpu.VMEM((16, wc), F32),
            pltpu.VMEM((16, wc), F32),
            pltpu.VMEM((tok, 128), F32),
            pltpu.VMEM((tok, 128), F32),
            pltpu.VMEM((tok, 128), BF16),
            pltpu.VMEM((16, width), F32),
            pltpu.VMEM((nl, 8, 128), F32),
            pltpu.VMEM((nq, 16, wc + 128), F32),
            pltpu.VMEM((nq, 16, wc + 128), F32),
            pltpu.VMEM((nl, 16, wc), BF16),
            pltpu.VMEM((nl, 16, wc), BF16),
            pltpu.VMEM((nq, 16, piece), F32),
            pltpu.VMEM((nq, 8, piece), F32),
            pltpu.VMEM((nq, 8, piece), F32),
            pltpu.VMEM((ng, 8, piece), F32),
            pltpu.VMEM((nq, 16, piece), F32),
            pltpu.VMEM((2, width), F32),
            pltpu.VMEM((1, 1), F32),
            pltpu.VMEM((16, feat + width), F32),
            dma((14,)),
            dma((8,)),
            dma((nl,)),
            dma((nl,)),
            dma((nq,)),
            dma((nq,)),
            dma((nl,)),
            dma((nl,)),
            dma((nq,)),
            dma((nq,)),
            dma((nl,)),
            dma((nl,)),
            dma,
            dma,
            dma((nq,)),
            dma((nq,)),
            dma((ng,)),
            dma((ng,)),
            dma((nq,)),
            dma((nq,)),
            dma,
            dma,
            dma((2, 2, 5, 4)),
            dma((2, 2, nq)),
            dma((2, nq)),
            dma((2, nq)),
            dma((nq,)),
            dma((nq,)),
        ],
        compiler_params=pltpu.CompilerParams(
            collective_id=0, has_side_effects=True, vmem_limit_bytes=56 * 1024 * 1024
        ),
    )(hidden, attn, weight, down.T, up, gain.reshape(1, width), queries, lengths, offsets, positives)
    attention, query, down_sum, up_sum, loss = results
    return attention, query, down_sum.T, up_sum, loss.reshape(())


def solution(mesh):
    ng = mesh.shape["grp"]
    nq = mesh.shape["dp"] // 2
    both = P(("grp", "dp"))
    rows = P(("grp", "dp"), None)
    return jax.shard_map(
        functools.partial(per_device, ng, nq),
        mesh=mesh,
        in_specs=(rows, rows, P("dp", None), P(), P(), P(), rows, both, both, both),
        out_specs=(rows, rows, P(), P(), P()),
        check_vma=False,
    )
```

```python
import functools

import jax
import jax.numpy as jnp
from jax import lax
from jax.experimental import pallas as pl
from jax.experimental.pallas import tpu as pltpu
from jax.sharding import PartitionSpec as P

MESH = pl.DeviceIdType.MESH
F32 = jnp.float32
BF16 = jnp.bfloat16
HI = lax.Precision.HIGHEST
NT = (((1,), (1,)), ((), ()))
TN = (((0,), (0,)), ((), ()))


def iota(shape, dim):
    return lax.broadcasted_iota(jnp.int32, shape, dim)


def mm(a, b, dims=None, precision=None):
    if dims is None:
        dims = (((1,), (0,)), ((), ()))
    return lax.dot_general(a, b, dims, precision=precision, preferred_element_type=F32)


def split3(x):
    high = x.astype(BF16).astype(F32)
    rest = x - high
    mid = rest.astype(BF16).astype(F32)
    return high, mid, (rest - mid).astype(BF16).astype(F32)


def kernel(
    ng,
    nq,
    hidden,
    attn,
    weight,
    down_h,
    up_h,
    gain_h,
    queries_h,
    lengths_h,
    offsets_h,
    positives_h,
    attn_out,
    query_out,
    down_out,
    up_out,
    loss_out,
    hv,
    av,
    wv,
    dyv,
    down_t,
    up,
    gain,
    queries,
    lengths,
    offsets,
    positives,
    ub,
    eb,
    unit_s,
    pool_s,
    ssq_s,
    col_s,
    bl_s,
    dn_s,
    lx,
    ll,
    dpb,
    rb,
    dub,
    rub,
    ab,
    core_in,
    plane_in,
    z_in,
    total_s,
    local_sem,
    u_sems,
    e_sems,
    x_sems,
    d_sems,
    v_sems,
    l_sems,
    c_send,
    c_recv,
    p_sems,
    z_sems,
    g_sems,
    s_send,
    s_recv,
    w_send,
    w_recv,
    wz_send,
    wz_recv,
    wc_send,
    wc_recv,
):
    nl = 2 * ng
    tok, width = hv.shape
    wc = width // 8
    feat = av.shape[1]
    passages = 2 * nl * nq
    middle = width // 2
    grp = lax.axis_index("grp")
    dp = lax.axis_index("dp")
    core = lax.rem(dp, 2)
    q_me = lax.div(dp, 2)
    l_me = 2 * grp + core

    def plane_peer(o):
        q = lax.rem(q_me + o, nq)
        return q, (grp, 2 * q + core)

    def line_peer(o):
        l = lax.rem(l_me + o, nl)
        return l, (lax.div(l, 2), 2 * q_me + lax.rem(l, 2))

    def z_peer(o):
        z = lax.rem(grp + o, ng)
        return z, (z, dp)

    def fan_out(n, peer, source, target, me, sems):
        def body(o, carry):
            there, device = peer(o)
            pltpu.make_async_remote_copy(
                src_ref=source(there),
                dst_ref=target.at[me],
                send_sem=sems.at[0],
                recv_sem=sems.at[1],
                device_id=device,
                device_id_type=MESH,
            ).start()
            return carry

        lax.fori_loop(1, n, body, 0)

    def amount(ref, sems):
        return pltpu.make_async_remote_copy(
            src_ref=ref,
            dst_ref=ref,
            send_sem=sems.at[0],
            recv_sem=sems.at[1],
            device_id=(grp, dp),
            device_id_type=MESH,
        )

    def fan_wait(n, target, sems):
        amount(target.at[0 : n - 1], sems).wait_recv()

    def fan_drain(n, target, sems):
        amount(target.at[0 : n - 1], sems).wait_send()

    def load(source, target, i):
        copy = pltpu.make_async_copy(source, target, local_sem.at[i])
        copy.start()
        return copy

    load_queries = load(queries_h, queries, 0)
    load_positives = load(positives_h, positives, 1)
    load_hidden = load(hidden, hv, 2)
    load_weight = load(weight, wv.at[dp], 3)
    load_rest = [
        load(gain_h, gain, 4),
        load(lengths_h, lengths, 5),
        load(offsets_h, offsets, 6),
    ]
    load_attn = load(attn, av, 7)
    load_down = load(down_h, down_t, 8)
    load_up = load(up_h, up, 9)

    barrier = pltpu.get_barrier_semaphore()

    def greet(n, peer):
        def body(o, carry):
            _, device = peer(o)
            pl.semaphore_signal(barrier, inc=1, device_id=device, device_id_type=MESH)
            return carry

        lax.fori_loop(1, n, body, 0)

    greet(nq, plane_peer)
    greet(nl, line_peer)

    x_me = lax.rem(q_me, 4)
    y_me = lax.div(q_me, 4)
    parity = lax.rem(grp, 2)

    def along(axis, o):
        if axis == 0:
            return 4 * y_me + lax.rem(x_me + o, 4)
        return 4 * lax.rem(y_me + o, 4) + x_me

    def w_rows(whose, part):
        return pl.ds(pl.multiple_of(32 * whose + 16 * part, 16), 16)

    def w_pieces(q, part, side):
        d = 2 * q + core
        first, last = ((0, 1), (0, 0.5), (0.5, 1))[side]

        def columns(start):
            size = width - start
            return pl.ds(start + int(first * size), int((last - first) * size))

        return (
            wv.at[d, w_rows(parity, part), columns(0)],
            wv.at[d, w_rows(1 - parity, part), columns(middle)],
        )

    def w_copy(q, part, axis, hop, side):
        for piece in w_pieces(q, part, side):
            pltpu.make_async_remote_copy(
                src_ref=piece,
                dst_ref=piece,
                send_sem=w_send.at[0 if side == 0 else 1],
                recv_sem=w_recv.at[part, side, q],
                device_id=(grp, 2 * along(axis, 1 if hop % 2 == 0 else 3) + core),
                device_id_type=MESH,
            ).start()

    def taken(ref, sem):
        return pltpu.make_async_remote_copy(
            src_ref=ref, dst_ref=ref, send_sem=sem, recv_sem=sem, device_id=(grp, dp), device_id_type=MESH
        )

    def w_wait_side(q, part, side):
        size = width // 2 if side == 0 else width // 4
        taken(wv.at[0, 0:48, 0:size], w_recv.at[part, side, q]).wait_recv()

    def at(oy, ox):
        return 4 * lax.rem(y_me + oy, 4) + lax.rem(x_me + ox, 4)

    def spot(part, o_first, o_second):
        return at(o_second, o_first) if part == 0 else at(o_first, o_second)

    def w_near(part, stage, o):
        axis = part if stage == 0 else 1 - part
        q = q_me if stage == 0 else spot(part, o, 0)
        for hop in (0, 1):
            w_copy(q, part, axis, hop, 0)

    def w_far(part, stage, o):
        axis = part if stage == 0 else 1 - part
        for hop, side, back_one in ((2, 1, 3), (3, 2, 1)):
            q = spot(part, back_one, 0) if stage == 0 else spot(part, o, back_one)
            w_copy(q, part, axis, hop, side)

    def w_wait(part, o_first, o_second):
        q = spot(part, o_first, o_second)
        last = o_first if o_second == 0 else o_second
        if last == 2:
            w_wait_side(q, part, 1)
            w_wait_side(q, part, 2)
        else:
            w_wait_side(q, part, 0)

    def z_copies(q):
        d = 2 * q + core
        for part, o in ((0, ng - 1), (1, 1)):
            piece = wv.at[d, w_rows(parity, part), 0:middle]
            yield pltpu.make_async_remote_copy(
                src_ref=piece,
                dst_ref=piece,
                send_sem=wz_send,
                recv_sem=wz_recv.at[q],
                device_id=(lax.rem(grp + o, ng), dp),
                device_id_type=MESH,
            )

    def w_across(q):
        for copy in z_copies(q):
            copy.start()

    def w_across_wait(q):
        taken(wv.at[0, 0:32, 0:middle], wz_recv.at[q]).wait_recv()

    def core_copies(q, side, pieces):
        d = 2 * q + side
        mine, rest = pl.ds(pl.multiple_of(32 * parity, 32), 32), pl.ds(pl.multiple_of(32 - 32 * parity, 32), 32)
        views = (
            wv.at[d, mine, :],
            wv.at[d, rest, middle:],
            wv.at[d, rest, 0:middle],
        )
        return [
            pltpu.make_async_remote_copy(
                src_ref=views[r],
                dst_ref=views[r],
                send_sem=wc_send,
                recv_sem=wc_recv.at[0 if r < 2 else 1, q],
                device_id=(grp, 2 * q_me + 1 - core),
                device_id_type=MESH,
            )
            for r in pieces
        ]

    def w_arrived(q):
        w_across(q)
        for copy in core_copies(q, core, (0, 1)):
            copy.start()

    def w_step0():
        load_weight.wait()
        for part in (0, 1):
            w_near(part, 0, 0)

    def w_step1():
        for part in (0, 1):
            w_near(part, 1, 0)
        for copy in core_copies(q_me, core, (0, 1, 2)):
            copy.start()
        for part in (0, 1):
            w_wait(part, 1, 0)
            w_wait(part, 3, 0)
            w_far(part, 0, 0)

    def w_step2():
        for part in (0, 1):
            w_near(part, 1, 1)
            w_near(part, 1, 3)
        for part in (0, 1):
            w_wait(part, 0, 1)
            w_wait(part, 0, 3)
        for oy, ox in ((0, 1), (0, 3), (1, 0), (3, 0)):
            w_arrived(at(oy, ox))

    def w_step3():
        for part in (0, 1):
            w_far(part, 1, 0)
            w_wait(part, 2, 0)
            w_near(part, 1, 2)
        for part in (0, 1):
            for o in (1, 3):
                w_wait(part, o, 1)
                w_wait(part, o, 3)
                w_far(part, 1, o)

    def w_step4():
        for part in (0, 1):
            w_wait(part, 2, 1)
            w_wait(part, 2, 3)
            w_far(part, 1, 2)
        for part in (0, 1):
            w_wait(part, 0, 2)
        for oy, ox in ((0, 2), (2, 0), (1, 1), (1, 3), (3, 1), (3, 3)):
            w_arrived(at(oy, ox))

    def w_step5():
        for part in (0, 1):
            w_wait(part, 1, 2)
            w_wait(part, 3, 2)
            w_wait(part, 2, 2)
        for oy, ox in ((1, 2), (3, 2), (2, 1), (2, 3), (2, 2)):
            w_arrived(at(oy, ox))

    def tile_at(t):
        def pick(values):
            out = values[0]
            for i, value in enumerate(values):
                out = jnp.where(t == i, value, out)
            return out

        oy = pick((0, 0, 1, 3, 1, 3, 2, 2))
        near = lax.div(x_me, 2)
        pair = lax.rem(near + pick((0, 1, 0, 0, 1, 1, 0, 1)), 2)
        return 2 * lax.rem(y_me + oy, 4) + pair

    def w_finish(q):
        w_across_wait(q)
        for copy in core_copies(q, core, (2,)):
            copy.start()

    def tile_start(t):
        n = tile_at(t)
        w_finish(2 * n)
        w_finish(2 * n + 1)

    def tile(t, carry):
        n = tile_at(t)
        for q in (2 * n, 2 * n + 1):
            taken(wv.at[0, 0:48, :], wc_recv.at[0, q]).wait_recv()
            taken(wv.at[0, 0:32, 0:middle], wc_recv.at[1, q]).wait_recv()
        columns = pl.ds(pl.multiple_of(256 * n, 256), 256)
        w_tile = wv[pl.ds(4 * n, 4)].reshape(256, width)
        out = mm(dyv[...], w_tile, NT) + mm(bl_s[:, 0:16], down_t[:, columns])
        attn_out[:, columns] = out.astype(BF16)
        return carry

    def w_drain():
        taken(wv.at[0:15, 0:32, :], w_send.at[0]).wait_send()
        taken(wv.at[0:15, 0:16, :], w_send.at[1]).wait_send()
        taken(wv.at[0:15, 0:16, :], wz_send).wait_send()
        taken(wv.at[0:16], wc_send).wait_send()

    odd16 = lax.rem(iota((16, 1), 0), 2) == 1

    def by_row(even, odd):
        return jnp.where(odd16, odd, even)

    def pair_sum(x):
        even = jnp.sum(jnp.where(odd16, 0.0, x), axis=0, keepdims=True)
        odd = jnp.sum(jnp.where(odd16, x, 0.0), axis=0, keepdims=True)
        return by_row(even, odd)

    def chunk(k):
        return slice(k * wc, (k + 1) * wc)

    load_queries.wait()
    load_positives.wait()
    for k in range(8):
        unit_s[2 * k : 2 * k + 2, :] = queries[:, chunk(k)].astype(F32)
    query16 = unit_s[...]
    qnorm = jnp.sqrt(pair_sum(jnp.sum(query16 * query16, axis=1, keepdims=True)) + 1e-06)
    unit16 = query16 / qnorm
    unit_s[...] = unit16
    ub[l_me, :, 0:wc] = unit16.astype(BF16)
    place = jnp.broadcast_to(by_row(positives[0], positives[1]), (16, 128))
    lane16 = iota((16, 128), 1)
    high_place = lax.shift_right_logical(place, 4)
    digits = jnp.where(lane16 == 0, high_place, jnp.where(lane16 == 1, place - 16 * high_place, 0))
    ub[l_me, :, wc:] = digits.astype(F32).astype(BF16)

    pl.semaphore_wait(barrier, nq - 1 + nl - 1)
    fan_out(nl, line_peer, lambda there: ub.at[l_me], ub, l_me, u_sems)
    w_step0()

    load_hidden.wait()

    def squares(i, carry):
        rows = pl.ds(pl.multiple_of(i * 16, 16), 16)
        v = hv[rows, :].astype(F32)
        v = v * v
        total = v[:, 0:128]
        for t in range(1, width // 128):
            total = total + v[:, t * 128 : t * 128 + 128]
        ssq_s[rows, :] = total
        return carry

    lax.fori_loop(0, tok // 16, squares, 0, unroll=2)
    ssq_row = mm(jnp.ones((8, 128), F32), ssq_s[...], NT, HI)[0:1, :]
    for copy in load_rest:
        copy.wait()
    rstd = lax.rsqrt(ssq_row * (1.0 / width) + 1e-05)
    token = iota((1, tok), 1)
    inside0 = (token >= offsets[0]) & (token < offsets[0] + lengths[0])
    inside1 = (token >= offsets[1]) & (token < offsets[1] + lengths[1])
    w0 = jnp.where(inside0, rstd, 0.0)
    w1 = jnp.where(inside1, rstd, 0.0)
    counts = by_row(lengths[0].astype(F32), lengths[1].astype(F32))
    row16 = iota((16, 1), 0)
    wh, wm, wl = split3(jnp.where(odd16, w1, w0))
    part = lax.div(row16, 2)
    w3 = jnp.where(part == 0, wh, jnp.where(part == 1, wm, jnp.where(part == 2, wl, 0.0))).astype(BF16)
    for k in range(8):
        p = mm(w3, hv[:, chunk(k)])
        pool_s[2 * k : 2 * k + 2, :] = (p[0:2] + p[2:4] + p[4:6]) * gain[0:1, chunk(k)]
    pooled = pool_s[...] / counts
    pnorm = jnp.sqrt(pair_sum(jnp.sum(pooled * pooled, axis=1, keepdims=True)) + 1e-06)
    embed = pooled / pnorm
    eb[q_me] = embed.astype(BF16)
    fan_out(nq, plane_peer, lambda there: eb.at[q_me], eb, q_me, e_sems)
    w_step1()

    load_attn.wait()
    load_down.wait()
    load_up.wait()
    flt = mm(down_t[...], av[...], NT).astype(BF16)
    hut = mm(up[...], hv[...], NT)
    na, nb = 16 * nq, 16 * nl
    np_, nqr = 2 * nq, 2 * nl

    def spread(rows, cols, row_is_block):
        small = iota((rows, cols), 0 if row_is_block else 1)
        big = iota((rows, cols), 1 if row_is_block else 0)
        return small == 2 * lax.div(big, 16) + lax.rem(big, 2)

    def as_f32(m):
        return jnp.where(m, 1.0, 0.0)

    same_chunk = lax.div(lax.rem(iota((na, nb), 0), 16), 2) == lax.div(lax.rem(iota((na, nb), 1), 16), 2)
    gather_a = as_f32(spread(np_, na, True))
    gather_b = as_f32(spread(nb, 128, False))
    first_b = as_f32(spread(nb, 128, False) & (lax.rem(iota((nb, 128), 0), 16) < 2))
    scatter_a = as_f32(spread(na, np_, False)).astype(BF16)
    scatter_b = as_f32(spread(128, nb, True)).astype(BF16)

    fan_wait(nl, ub, u_sems)
    ubm = ub[:, :, 0:wc].reshape(nb, wc)
    digit = as_f32(iota((16, 128), 0) == iota((16, 128), 1)).astype(BF16)
    place_b = mm(digit, ub[:, :, wc:].reshape(nb, 128), NT).astype(BF16)
    place_i = mm(place_b, first_b.astype(BF16))
    pos = 16.0 * place_i[0:1, :] + place_i[1:2, :]
    passage = iota((np_, 1), 0)
    number = 2 * (grp * 2 * nq + 2 * lax.div(passage, 2) + core) + lax.rem(passage, 2)
    used = iota((1, 128), 1) < nqr
    target = jnp.where((number.astype(F32) == pos) & used, 1.0, 0.0)

    fan_wait(nq, eb, e_sems)
    ebm = eb[...].reshape(na, wc)
    products = jnp.where(same_chunk, mm(ebm, ubm, NT), 0.0)
    logits = 50.0 * mm(mm(gather_a, products, precision=HI), gather_b, precision=HI)
    expo = jnp.where(used, jnp.exp(logits), 0.0)
    partial = jnp.sum(expo, axis=0, keepdims=True)
    chosen = jnp.sum(logits * target, axis=0, keepdims=True)
    row8 = iota((8, 128), 0)
    lx[l_me] = jnp.where(row8 == 0, partial, jnp.where(row8 == 1, chosen, 0.0))
    fan_out(nl, line_peer, lambda there: lx.at[l_me], lx, l_me, x_sems)
    w_step2()
    fan_wait(nl, lx, x_sems)
    line = jnp.sum(lx[...], axis=0)
    lse = jnp.log(jnp.where(used, line[0:1, :], 1.0))
    line_loss = jnp.sum(jnp.where(used, lse - line[1:2, :], 0.0), axis=1, keepdims=True)
    prob = jnp.exp(logits - lse)
    grad = jnp.where(used, (prob - target) * 1024.0, 0.0).astype(BF16)
    spread_grad = mm(mm(scatter_a, grad).astype(BF16), scatter_b)
    g1 = jnp.where(same_chunk, spread_grad, 0.0)
    dpb[...] = mm(g1.astype(BF16), ubm).reshape(nq, 16, wc).astype(BF16)
    rb[q_me] = dpb[q_me]
    fan_out(nq, plane_peer, lambda there: dpb.at[there], rb, q_me, d_sems)
    ll[q_me] = jnp.broadcast_to(line_loss, (8, 128))
    fan_out(nq, plane_peer, lambda there: ll.at[q_me], ll, q_me, l_sems)
    w_step3()
    dub[...] = mm(jnp.transpose(g1).astype(BF16), ebm).reshape(nl, 16, wc).astype(BF16)
    rub[l_me] = dub[l_me]
    fan_out(nl, line_peer, lambda there: dub.at[there], rub, l_me, v_sems)

    fan_wait(nq, rb, d_sems)
    d_embed = 50.0 * jnp.sum(rb[...].astype(F32), axis=0)
    shared = pair_sum(jnp.sum(embed * d_embed, axis=1, keepdims=True))
    pool_s[...] = (d_embed - embed * shared) / pnorm / counts
    dn_s[...] = jnp.zeros_like(dn_s)
    for k in range(8):
        dn = pool_s[2 * k : 2 * k + 2, :] * gain[0:1, chunk(k)]
        dh, dm, dl = split3(dn)
        dn_s[0:2, chunk(k)] = dh
        dn_s[2:4, chunk(k)] = dm
        dn_s[4:6, chunk(k)] = dl
        dn_s[8:10, chunk(k)] = dn
    dn3 = jnp.where(row16 < 6, dn_s[...], 0.0).astype(BF16)

    s3 = mm(dn3, hv[...], NT)
    s0 = s3[0:1] + s3[2:3] + s3[4:5]
    s1 = s3[1:2] + s3[3:4] + s3[5:6]
    s = jnp.where(inside0, s0, jnp.where(inside1, s1, 0.0))
    b = rstd * rstd * rstd * s * (1.0 / width)
    u3 = mm(up[...], dn3, NT)
    u0 = u3[:, 0:1] + u3[:, 2:3] + u3[:, 4:5]
    u1 = u3[:, 1:2] + u3[:, 3:4] + u3[:, 5:6]
    blt = (2.0 * (u0 * w0 + u1 * w1 - b * hut)).astype(BF16)
    tiles_down, tiles_up = feat // 128, width // 128
    per = (tiles_down + tiles_up) // nq

    def put(t, x):
        ab[t // per, :, (t % per) * 128 : (t % per) * 128 + 128] = x

    def get(ref, t):
        return ref[t // per, :, (t % per) * 128 : (t % per) * 128 + 128]

    down_part = mm(blt, av[...])
    for t in range(tiles_down):
        put(t, down_part[:, t * 128 : t * 128 + 128])
    fl = flt.astype(F32)
    fb = b * fl
    fbh = fb.astype(BF16)
    fbl = (fb - fbh.astype(F32)).astype(BF16)
    f0 = jnp.sum(w0 * fl, axis=1, keepdims=True)
    f1 = jnp.sum(w1 * fl, axis=1, keepdims=True)
    fb2 = jnp.concatenate([fbh, fbl], axis=0)
    for k in range(8):
        up2 = mm(fb2, hv[:, chunk(k)])
        up2 = up2[0:16] + up2[16:32]
        up_part = 2.0 * (f0 * dn_s[8:9, chunk(k)] + f1 * dn_s[9:10, chunk(k)] - up2)
        for t in range(wc // 128):
            put(tiles_down + k * (wc // 128) + t, up_part[:, t * 128 : t * 128 + 128])

    def half(which):
        return pl.ds(pl.multiple_of(8 * which, 8), 8)

    other = 1 - core
    swap = pltpu.make_async_remote_copy(
        src_ref=ab.at[:, half(other), :],
        dst_ref=core_in,
        send_sem=c_send,
        recv_sem=c_recv,
        device_id=(grp, 2 * q_me + other),
        device_id_type=MESH,
    )
    swap.start()

    swap.wait_recv()
    mine = half(core)
    core_in[...] = core_in[...] + ab[:, mine, :]
    plane_in[q_me] = core_in[q_me]
    fan_out(nq, plane_peer, lambda there: core_in.at[there], plane_in, q_me, p_sems)
    w_step4()

    row_id = iota((128, tok), 0)
    col_s[...] = jnp.transpose(jnp.where(row_id == 0, w0 + w1, jnp.where(row_id == 1, b, 0.0)))
    blf = jnp.concatenate([blt.astype(F32), jnp.zeros((112, tok), F32)], axis=0)
    bl_s[...] = jnp.transpose(blf).astype(BF16)

    def rows_dy(i, carry):
        rows = pl.ds(pl.multiple_of(i * 16, 16), 16)
        c = col_s[rows, :]
        second = jnp.where(i * 16 >= offsets[1], 1, 0)
        dn_row = dn_s[pl.ds(8 + second, 1), :]
        dyv[rows, :] = (c[:, 0:1] * dn_row - c[:, 1:2] * hv[rows, :].astype(F32)).astype(BF16)
        return carry

    lax.fori_loop(0, tok // 16, rows_dy, 0, unroll=2)

    fan_wait(nq, plane_in, p_sems)
    z_in[grp] = jnp.sum(plane_in[...], axis=0)
    fan_out(ng, z_peer, lambda there: z_in.at[grp], z_in, grp, z_sems)
    w_step5()

    fan_wait(nl, rub, v_sems)
    d_unit = 50.0 * jnp.sum(rub[...].astype(F32), axis=0)
    unit = unit_s[...]
    unit_s[...] = (d_unit - unit * pair_sum(jnp.sum(unit * d_unit, axis=1, keepdims=True))) / qnorm
    for k in range(8):
        query_out[:, chunk(k)] = unit_s[2 * k : 2 * k + 2, :]
    fan_wait(nq, ll, l_sems)
    loss_out[...] = jnp.sum(ll[...], axis=0)[0:1, 0:1] * (1.0 / passages)
    w_finish(4 * y_me + x_me + 1 - 2 * lax.rem(x_me, 2))
    tile_start(1)
    tile(0, 0)
    tile_start(2)
    tile(1, 0)

    fan_wait(ng, z_in, z_sems)
    total_s[q_me, mine, :] = jnp.sum(z_in[...], axis=0)

    def gather_piece(o, carry):
        there, device = plane_peer(o)
        pltpu.make_async_remote_copy(
            src_ref=total_s.at[q_me, mine, :],
            dst_ref=total_s.at[q_me, mine, :],
            send_sem=g_sems.at[0],
            recv_sem=g_sems.at[1],
            device_id=device,
            device_id_type=MESH,
        ).start()
        return carry

    lax.fori_loop(1, nq, gather_piece, 0)
    tile_start(3)
    tile(2, 0)
    tile_start(4)
    tile(3, 0)
    amount(total_s.at[0 : nq - 1, mine, :], g_sems).wait_recv()
    back = pltpu.make_async_remote_copy(
        src_ref=total_s.at[:, mine, :],
        dst_ref=total_s.at[:, mine, :],
        send_sem=s_send,
        recv_sem=s_recv,
        device_id=(grp, 2 * q_me + other),
        device_id_type=MESH,
    )
    back.start()

    def tiles(t, carry):
        tile_start(t + 1)
        return tile(t, carry)

    lax.fori_loop(4, 7, tiles, 0)
    tile(7, 0)

    back.wait_recv()
    for t in range(tiles_down):
        down_out[:, t * 128 : t * 128 + 128] = get(total_s, t)
    for t in range(tiles_up):
        up_out[:, t * 128 : t * 128 + 128] = get(total_s, tiles_down + t)
    fan_drain(nl, ub, u_sems)
    fan_drain(nq, eb, e_sems)
    fan_drain(nl, lx, x_sems)
    fan_drain(nq, dpb, d_sems)
    fan_drain(nq, ll, l_sems)
    fan_drain(nl, dub, v_sems)
    fan_drain(nq, core_in, p_sems)
    fan_drain(ng, z_in, z_sems)
    amount(total_s.at[0 : nq - 1, mine, :], g_sems).wait_send()
    swap.wait_send()
    back.wait_send()
    w_drain()


def finish(*refs):
    count = len(refs) // 2
    copies = []
    rows = refs[0].shape[0] // 8
    for i in range(8):
        part = pl.ds(i * rows, rows)
        copies.append(pltpu.make_async_copy(refs[0].at[part, :], refs[count].at[part, :], refs[-1].at[i]))
    for i in range(1, count):
        copies.append(pltpu.make_async_copy(refs[i], refs[count + i], refs[-1].at[7 + i]))
    for copy in copies:
        copy.start()
    for copy in copies:
        copy.wait()


def per_device(ng, nq, attn, hidden, weight, down, up, gain, queries, lengths, offsets, positives):
    tok, width = hidden.shape
    feat = attn.shape[1]
    wc = width // 8
    nl = 2 * ng
    piece = (feat + width) // nq
    vmem = pl.BlockSpec(memory_space=pltpu.VMEM)
    hbm = pl.BlockSpec(memory_space=pltpu.HBM)
    dma = pltpu.SemaphoreType.DMA
    outs = (
        jax.ShapeDtypeStruct((tok, feat), BF16),
        jax.ShapeDtypeStruct((2, width), F32),
        jax.ShapeDtypeStruct((16, feat), F32),
        jax.ShapeDtypeStruct((16, width), F32),
        jax.ShapeDtypeStruct((1, 1), F32),
    )
    results = pl.pallas_call(
        functools.partial(kernel, ng, nq),
        out_shape=outs,
        in_specs=[hbm] * 10,
        out_specs=(vmem,) * 5,
        scratch_shapes=[
            pltpu.VMEM((tok, width), BF16),
            pltpu.VMEM((tok, feat), BF16),
            pltpu.VMEM((2 * nq, 64, width), BF16),
            pltpu.VMEM((tok, width), BF16),
            pltpu.VMEM((16, feat), BF16),
            pltpu.VMEM((16, width), BF16),
            pltpu.VMEM((1, width), F32),
            pltpu.VMEM((2, width), BF16),
            pltpu.SMEM((2,), jnp.int32),
            pltpu.SMEM((2,), jnp.int32),
            pltpu.SMEM((2,), jnp.int32),
            pltpu.VMEM((nl, 16, wc + 128), BF16),
            pltpu.VMEM((nq, 16, wc), BF16),
            pltpu.VMEM((16, wc), F32),
            pltpu.VMEM((16, wc), F32),
            pltpu.VMEM((tok, 128), F32),
            pltpu.VMEM((tok, 128), F32),
            pltpu.VMEM((tok, 128), BF16),
            pltpu.VMEM((16, width), F32),
            pltpu.VMEM((nl, 8, 128), F32),
            pltpu.VMEM((nq, 8, 128), F32),
            pltpu.VMEM((nq, 16, wc), BF16),
            pltpu.VMEM((nq, 16, wc), BF16),
            pltpu.VMEM((nl, 16, wc), BF16),
            pltpu.VMEM((nl, 16, wc), BF16),
            pltpu.VMEM((nq, 16, piece), F32),
            pltpu.VMEM((nq, 8, piece), F32),
            pltpu.VMEM((nq, 8, piece), F32),
            pltpu.VMEM((ng, 8, piece), F32),
            pltpu.VMEM((nq, 16, piece), F32),
            dma((10,)),
            dma((2,)),
            dma((2,)),
            dma((2,)),
            dma((2,)),
            dma((2,)),
            dma((2,)),
            dma,
            dma,
            dma((2,)),
            dma((2,)),
            dma((2,)),
            dma,
            dma,
            dma((2,)),
            dma((2, 3, nq)),
            dma,
            dma((nq,)),
            dma,
            dma((2, nq)),
        ],
        compiler_params=pltpu.CompilerParams(
            collective_id=0, has_side_effects=True, vmem_limit_bytes=56 * 1024 * 1024
        ),
    )(hidden, attn, weight, down.T, up, gain.reshape(1, width), queries, lengths, offsets, positives)
    attention, query, down_sum, up_sum, loss = pl.pallas_call(
        finish,
        out_shape=outs,
        in_specs=[vmem] * 5,
        out_specs=(hbm,) * 5,
        scratch_shapes=[dma((12,))],
    )(*results)
    return attention, query, down_sum.T, up_sum, loss.reshape(())


def solution(mesh):
    ng = mesh.shape["grp"]
    nq = mesh.shape["dp"] // 2
    both = P(("grp", "dp"))
    rows = P(("grp", "dp"), None)
    return jax.shard_map(
        functools.partial(per_device, ng, nq),
        mesh=mesh,
        in_specs=(rows, rows, P("dp", None), P(), P(), P(), rows, both, both, both),
        out_specs=(rows, rows, P(), P(), P()),
        check_vma=False,
    )
```

```python
import functools

import jax
import jax.numpy as jnp
from jax import lax
from jax.experimental import pallas as pl
from jax.experimental.pallas import tpu as pltpu
from jax.sharding import PartitionSpec as P

MESH = pl.DeviceIdType.MESH
F32 = jnp.float32
BF16 = jnp.bfloat16
HI = lax.Precision.HIGHEST
NT = (((1,), (1,)), ((), ()))
TN = (((0,), (0,)), ((), ()))


def iota(shape, dim):
    return lax.broadcasted_iota(jnp.int32, shape, dim)


def mm(a, b, dims=None, precision=None):
    if dims is None:
        dims = (((1,), (0,)), ((), ()))
    return lax.dot_general(a, b, dims, precision=precision, preferred_element_type=F32)


def split3(x):
    high = x.astype(BF16).astype(F32)
    rest = x - high
    mid = rest.astype(BF16).astype(F32)
    return high, mid, (rest - mid).astype(BF16).astype(F32)


def kernel(
    ng,
    nq,
    hidden,
    attn,
    weight,
    down_h,
    up_h,
    gain_h,
    queries_h,
    lengths_h,
    offsets_h,
    positives_h,
    attn_out,
    query_out,
    down_out,
    up_out,
    loss_out,
    hv,
    av,
    wv,
    dyv,
    ov,
    query_s,
    down_s,
    up_s,
    loss_s,
    down_t,
    up,
    gain,
    queries,
    lengths,
    offsets,
    positives,
    ub,
    eb,
    unit_s,
    pool_s,
    ssq_s,
    col_s,
    bl_s,
    dn_s,
    lx,
    ll,
    dpb,
    rb,
    dub,
    rub,
    ab,
    core_in,
    plane_in,
    z_in,
    total_s,
    local_sem,
    out_sem,
    u_sems,
    e_sems,
    x_sems,
    d_sems,
    v_sems,
    l_sems,
    c_send,
    c_recv,
    p_sems,
    z_sems,
    g_sems,
    s_send,
    s_recv,
    w_send,
    w_recv,
    wz_send,
    wz_recv,
    wc_send,
    wc_recv,
):
    nl = 2 * ng
    tok, width = hv.shape
    wc = width // 8
    feat = av.shape[1]
    passages = 2 * nl * nq
    middle = width // 2
    grp = lax.axis_index("grp")
    dp = lax.axis_index("dp")
    core = lax.rem(dp, 2)
    q_me = lax.div(dp, 2)
    l_me = 2 * grp + core

    def plane_peer(o):
        q = lax.rem(q_me + o, nq)
        return q, (grp, 2 * q + core)

    def line_peer(o):
        l = lax.rem(l_me + o, nl)
        return l, (lax.div(l, 2), 2 * q_me + lax.rem(l, 2))

    def z_peer(o):
        z = lax.rem(grp + o, ng)
        return z, (z, dp)

    def fan_out(n, peer, source, target, me, sems):
        def body(o, carry):
            there, device = peer(o)
            pltpu.make_async_remote_copy(
                src_ref=source(there),
                dst_ref=target.at[me],
                send_sem=sems.at[0],
                recv_sem=sems.at[1],
                device_id=device,
                device_id_type=MESH,
            ).start()
            return carry

        lax.fori_loop(1, n, body, 0)

    def amount(ref, sems):
        return pltpu.make_async_remote_copy(
            src_ref=ref,
            dst_ref=ref,
            send_sem=sems.at[0],
            recv_sem=sems.at[1],
            device_id=(grp, dp),
            device_id_type=MESH,
        )

    def fan_wait(n, target, sems):
        amount(target.at[0 : n - 1], sems).wait_recv()

    def fan_drain(n, target, sems):
        amount(target.at[0 : n - 1], sems).wait_send()

    def load(source, target, i):
        copy = pltpu.make_async_copy(source, target, local_sem.at[i])
        copy.start()
        return copy

    load_queries = load(queries_h, queries, 0)
    load_positives = load(positives_h, positives, 1)
    load_hidden = load(hidden, hv, 2)
    load_weight = load(weight, wv.at[dp], 3)
    load_rest = [
        load(gain_h, gain, 4),
        load(lengths_h, lengths, 5),
        load(offsets_h, offsets, 6),
    ]
    load_attn = load(attn, av, 7)
    load_down = load(down_h, down_t, 8)
    load_up = load(up_h, up, 9)

    barrier = pltpu.get_barrier_semaphore()

    def greet(n, peer):
        def body(o, carry):
            _, device = peer(o)
            pl.semaphore_signal(barrier, inc=1, device_id=device, device_id_type=MESH)
            return carry

        lax.fori_loop(1, n, body, 0)

    greet(nq, plane_peer)
    greet(nl, line_peer)

    x_me = lax.rem(q_me, 4)
    y_me = lax.div(q_me, 4)
    parity = lax.rem(grp, 2)

    def along(axis, o):
        if axis == 0:
            return 4 * y_me + lax.rem(x_me + o, 4)
        return 4 * lax.rem(y_me + o, 4) + x_me

    def w_rows(whose, part):
        return pl.ds(pl.multiple_of(32 * whose + 16 * part, 16), 16)

    def w_pieces(q, part, side):
        d = 2 * q + core
        first, last = ((0, 1), (0, 0.5), (0.5, 1))[side]

        def columns(start):
            size = width - start
            return pl.ds(start + int(first * size), int((last - first) * size))

        return (
            wv.at[d, w_rows(parity, part), columns(0)],
            wv.at[d, w_rows(1 - parity, part), columns(middle)],
        )

    def w_copy(q, part, axis, hop, side):
        for piece in w_pieces(q, part, side):
            pltpu.make_async_remote_copy(
                src_ref=piece,
                dst_ref=piece,
                send_sem=w_send.at[0 if side == 0 else 1],
                recv_sem=w_recv.at[part, side, q],
                device_id=(grp, 2 * along(axis, 1 if hop % 2 == 0 else 3) + core),
                device_id_type=MESH,
            ).start()

    def taken(ref, sem):
        return pltpu.make_async_remote_copy(
            src_ref=ref, dst_ref=ref, send_sem=sem, recv_sem=sem, device_id=(grp, dp), device_id_type=MESH
        )

    def w_wait_side(q, part, side):
        size = width // 2 if side == 0 else width // 4
        taken(wv.at[0, 0:48, 0:size], w_recv.at[part, side, q]).wait_recv()

    def at(oy, ox):
        return 4 * lax.rem(y_me + oy, 4) + lax.rem(x_me + ox, 4)

    def spot(part, o_first, o_second):
        return at(o_second, o_first) if part == 0 else at(o_first, o_second)

    def w_near(part, stage, o):
        axis = part if stage == 0 else 1 - part
        q = q_me if stage == 0 else spot(part, o, 0)
        for hop in (0, 1):
            w_copy(q, part, axis, hop, 0)

    def w_far(part, stage, o):
        axis = part if stage == 0 else 1 - part
        for hop, side, back_one in ((2, 1, 3), (3, 2, 1)):
            q = spot(part, back_one, 0) if stage == 0 else spot(part, o, back_one)
            w_copy(q, part, axis, hop, side)

    def w_wait(part, o_first, o_second):
        q = spot(part, o_first, o_second)
        last = o_first if o_second == 0 else o_second
        if last == 2:
            w_wait_side(q, part, 1)
            w_wait_side(q, part, 2)
        else:
            w_wait_side(q, part, 0)

    def z_copies(q):
        d = 2 * q + core
        for part, o in ((0, ng - 1), (1, 1)):
            piece = wv.at[d, w_rows(parity, part), 0:middle]
            yield pltpu.make_async_remote_copy(
                src_ref=piece,
                dst_ref=piece,
                send_sem=wz_send,
                recv_sem=wz_recv.at[q],
                device_id=(lax.rem(grp + o, ng), dp),
                device_id_type=MESH,
            )

    def w_across(q):
        for copy in z_copies(q):
            copy.start()

    def w_across_wait(q):
        taken(wv.at[0, 0:32, 0:middle], wz_recv.at[q]).wait_recv()

    def core_copies(q, side, pieces):
        d = 2 * q + side
        mine, rest = pl.ds(pl.multiple_of(32 * parity, 32), 32), pl.ds(pl.multiple_of(32 - 32 * parity, 32), 32)
        views = (
            wv.at[d, mine, :],
            wv.at[d, rest, middle:],
            wv.at[d, rest, 0:middle],
        )
        return [
            pltpu.make_async_remote_copy(
                src_ref=views[r],
                dst_ref=views[r],
                send_sem=wc_send,
                recv_sem=wc_recv.at[0 if r < 2 else 1, q],
                device_id=(grp, 2 * q_me + 1 - core),
                device_id_type=MESH,
            )
            for r in pieces
        ]

    def w_arrived(q):
        w_across(q)
        for copy in core_copies(q, core, (0, 1)):
            copy.start()

    def w_step0():
        load_weight.wait()
        for part in (0, 1):
            w_near(part, 0, 0)

    def w_step1():
        for part in (0, 1):
            w_near(part, 1, 0)
        for copy in core_copies(q_me, core, (0, 1, 2)):
            copy.start()
        for part in (0, 1):
            w_wait(part, 1, 0)
            w_wait(part, 3, 0)
            w_far(part, 0, 0)

    def w_step2():
        for part in (0, 1):
            w_near(part, 1, 1)
            w_near(part, 1, 3)
        for part in (0, 1):
            w_wait(part, 0, 1)
            w_wait(part, 0, 3)
        for oy, ox in ((0, 1), (0, 3), (1, 0), (3, 0)):
            w_arrived(at(oy, ox))

    def w_step3():
        for part in (0, 1):
            w_wait(part, 2, 0)
            w_near(part, 1, 2)
            w_far(part, 1, 0)
        for part in (0, 1):
            for o in (1, 3):
                w_wait(part, o, 1)
                w_wait(part, o, 3)
                w_far(part, 1, o)
        for oy, ox in ((1, 1), (1, 3), (3, 1), (3, 3)):
            w_arrived(at(oy, ox))

    def w_step4():
        for part in (0, 1):
            w_wait(part, 0, 2)
        for oy, ox in ((0, 2), (2, 0)):
            w_arrived(at(oy, ox))

    def w_step45():
        for part in (0, 1):
            w_wait(part, 2, 1)
            w_wait(part, 2, 3)
            w_far(part, 1, 2)

    def w_step5():
        for part in (0, 1):
            w_wait(part, 1, 2)
            w_wait(part, 3, 2)
        for oy, ox in ((1, 2), (3, 2), (2, 1), (2, 3)):
            w_arrived(at(oy, ox))

    def w_step6():
        for part in (0, 1):
            w_wait(part, 2, 2)
        w_arrived(at(2, 2))

    def tile_at(t):
        def pick(values):
            out = values[0]
            for i, value in enumerate(values):
                out = jnp.where(t == i, value, out)
            return out

        oy = pick((0, 0, 1, 3, 1, 3, 2, 2))
        near = lax.div(x_me, 2)
        pair = lax.rem(near + pick((0, 1, 0, 0, 1, 1, 0, 1)), 2)
        return 2 * lax.rem(y_me + oy, 4) + pair

    def w_finish(q):
        w_across_wait(q)
        for copy in core_copies(q, core, (2,)):
            copy.start()

    def tile_start(t):
        n = tile_at(t)
        w_finish(2 * n)
        w_finish(2 * n + 1)

    def tile(t, carry):
        n = tile_at(t)
        for q in (2 * n, 2 * n + 1):
            taken(wv.at[0, 0:48, :], wc_recv.at[0, q]).wait_recv()
            taken(wv.at[0, 0:32, 0:middle], wc_recv.at[1, q]).wait_recv()
        columns = pl.ds(pl.multiple_of(256 * n, 256), 256)
        w_tile = wv[pl.ds(4 * n, 4)].reshape(256, width)
        out = mm(dyv[...], w_tile, NT) + mm(bl_s[:, 0:16], down_t[:, columns])
        ov[:, columns] = out.astype(BF16)
        pltpu.make_async_copy(ov.at[:, columns], attn_out.at[:, columns], out_sem.at[t]).start()
        return carry

    def tile_stored(t, carry):
        columns = pl.ds(pl.multiple_of(256 * tile_at(t), 256), 256)
        pltpu.make_async_copy(ov.at[:, columns], attn_out.at[:, columns], out_sem.at[t]).wait()
        return carry

    def store(source, target, i):
        copy = pltpu.make_async_copy(source, target, local_sem.at[i])
        copy.start()
        return copy

    def w_drain():
        taken(wv.at[0:15, 0:32, :], w_send.at[0]).wait_send()
        taken(wv.at[0:15, 0:16, :], w_send.at[1]).wait_send()
        taken(wv.at[0:15, 0:16, :], wz_send).wait_send()
        taken(wv.at[0:16], wc_send).wait_send()

    odd16 = lax.rem(iota((16, 1), 0), 2) == 1

    def by_row(even, odd):
        return jnp.where(odd16, odd, even)

    def pair_sum(x):
        even = jnp.sum(jnp.where(odd16, 0.0, x), axis=0, keepdims=True)
        odd = jnp.sum(jnp.where(odd16, x, 0.0), axis=0, keepdims=True)
        return by_row(even, odd)

    def chunk(k):
        return slice(k * wc, (k + 1) * wc)

    load_queries.wait()
    load_positives.wait()
    for k in range(8):
        unit_s[2 * k : 2 * k + 2, :] = queries[:, chunk(k)].astype(F32)
    query16 = unit_s[...]
    qnorm = jnp.sqrt(pair_sum(jnp.sum(query16 * query16, axis=1, keepdims=True)) + 1e-06)
    unit16 = query16 / qnorm
    unit_s[...] = unit16
    ub[l_me, :, 0:wc] = unit16.astype(BF16)
    place = jnp.broadcast_to(by_row(positives[0], positives[1]), (16, 128))
    lane16 = iota((16, 128), 1)
    high_place = lax.shift_right_logical(place, 4)
    digits = jnp.where(lane16 == 0, high_place, jnp.where(lane16 == 1, place - 16 * high_place, 0))
    ub[l_me, :, wc:] = digits.astype(F32).astype(BF16)

    pl.semaphore_wait(barrier, nq - 1 + nl - 1)
    fan_out(nl, line_peer, lambda there: ub.at[l_me], ub, l_me, u_sems)
    w_step0()

    load_hidden.wait()

    def squares(i, carry):
        rows = pl.ds(pl.multiple_of(i * 16, 16), 16)
        v = hv[rows, :].astype(F32)
        v = v * v
        total = v[:, 0:128]
        for t in range(1, width // 128):
            total = total + v[:, t * 128 : t * 128 + 128]
        ssq_s[rows, :] = total
        return carry

    lax.fori_loop(0, tok // 16, squares, 0, unroll=2)
    ssq_row = mm(jnp.ones((8, 128), F32), ssq_s[...], NT, HI)[0:1, :]
    for copy in load_rest:
        copy.wait()
    rstd = lax.rsqrt(ssq_row * (1.0 / width) + 1e-05)
    token = iota((1, tok), 1)
    inside0 = (token >= offsets[0]) & (token < offsets[0] + lengths[0])
    inside1 = (token >= offsets[1]) & (token < offsets[1] + lengths[1])
    w0 = jnp.where(inside0, rstd, 0.0)
    w1 = jnp.where(inside1, rstd, 0.0)
    counts = by_row(lengths[0].astype(F32), lengths[1].astype(F32))
    row16 = iota((16, 1), 0)
    wh, wm, wl = split3(jnp.where(odd16, w1, w0))
    part = lax.div(row16, 2)
    w3 = jnp.where(part == 0, wh, jnp.where(part == 1, wm, jnp.where(part == 2, wl, 0.0))).astype(BF16)
    for k in range(8):
        p = mm(w3, hv[:, chunk(k)])
        pool_s[2 * k : 2 * k + 2, :] = (p[0:2] + p[2:4] + p[4:6]) * gain[0:1, chunk(k)]
    pooled = pool_s[...] / counts
    pnorm = jnp.sqrt(pair_sum(jnp.sum(pooled * pooled, axis=1, keepdims=True)) + 1e-06)
    embed = pooled / pnorm
    eb[q_me] = embed.astype(BF16)
    fan_out(nq, plane_peer, lambda there: eb.at[q_me], eb, q_me, e_sems)
    w_step1()

    load_attn.wait()
    load_down.wait()
    load_up.wait()
    flt = mm(down_t[...], av[...], NT).astype(BF16)
    hut = mm(up[...], hv[...], NT)
    na, nb = 16 * nq, 16 * nl
    np_, nqr = 2 * nq, 2 * nl

    def spread(rows, cols, row_is_block):
        small = iota((rows, cols), 0 if row_is_block else 1)
        big = iota((rows, cols), 1 if row_is_block else 0)
        return small == 2 * lax.div(big, 16) + lax.rem(big, 2)

    def as_f32(m):
        return jnp.where(m, 1.0, 0.0)

    same_chunk = lax.div(lax.rem(iota((na, nb), 0), 16), 2) == lax.div(lax.rem(iota((na, nb), 1), 16), 2)
    gather_a = as_f32(spread(np_, na, True))
    gather_b = as_f32(spread(nb, 128, False))
    first_b = as_f32(spread(nb, 128, False) & (lax.rem(iota((nb, 128), 0), 16) < 2))
    scatter_a = as_f32(spread(na, np_, False)).astype(BF16)
    scatter_b = as_f32(spread(128, nb, True)).astype(BF16)

    fan_wait(nl, ub, u_sems)
    ubm = ub[:, :, 0:wc].reshape(nb, wc)
    digit = as_f32(iota((16, 128), 0) == iota((16, 128), 1)).astype(BF16)
    place_b = mm(digit, ub[:, :, wc:].reshape(nb, 128), NT).astype(BF16)
    place_i = mm(place_b, first_b.astype(BF16))
    pos = 16.0 * place_i[0:1, :] + place_i[1:2, :]
    passage = iota((np_, 1), 0)
    number = 2 * (grp * 2 * nq + 2 * lax.div(passage, 2) + core) + lax.rem(passage, 2)
    used = iota((1, 128), 1) < nqr
    target = jnp.where((number.astype(F32) == pos) & used, 1.0, 0.0)

    fan_wait(nq, eb, e_sems)
    ebm = eb[...].reshape(na, wc)
    products = jnp.where(same_chunk, mm(ebm, ubm, NT), 0.0)
    logits = 50.0 * mm(mm(gather_a, products, precision=HI), gather_b, precision=HI)
    expo = jnp.where(used, jnp.exp(logits), 0.0)
    partial = jnp.sum(expo, axis=0, keepdims=True)
    chosen = jnp.sum(logits * target, axis=0, keepdims=True)
    row8 = iota((8, 128), 0)
    lx[l_me] = jnp.where(row8 == 0, partial, jnp.where(row8 == 1, chosen, 0.0))
    fan_out(nl, line_peer, lambda there: lx.at[l_me], lx, l_me, x_sems)
    w_step2()
    fan_wait(nl, lx, x_sems)
    line = jnp.sum(lx[...], axis=0)
    lse = jnp.log(jnp.where(used, line[0:1, :], 1.0))
    line_loss = jnp.sum(jnp.where(used, lse - line[1:2, :], 0.0), axis=1, keepdims=True)
    prob = jnp.exp(logits - lse)
    grad = jnp.where(used, (prob - target) * 1024.0, 0.0).astype(BF16)
    spread_grad = mm(mm(scatter_a, grad).astype(BF16), scatter_b)
    g1 = jnp.where(same_chunk, spread_grad, 0.0)
    dpb[...] = mm(g1.astype(BF16), ubm).reshape(nq, 16, wc).astype(BF16)
    rb[q_me] = dpb[q_me]
    fan_out(nq, plane_peer, lambda there: dpb.at[there], rb, q_me, d_sems)
    ll[q_me] = jnp.broadcast_to(line_loss, (8, 128))
    fan_out(nq, plane_peer, lambda there: ll.at[q_me], ll, q_me, l_sems)
    w_step3()
    dub[...] = mm(jnp.transpose(g1).astype(BF16), ebm).reshape(nl, 16, wc).astype(BF16)
    rub[l_me] = dub[l_me]
    fan_out(nl, line_peer, lambda there: dub.at[there], rub, l_me, v_sems)

    w_step4()
    fan_wait(nq, rb, d_sems)
    w_step45()
    d_embed = 50.0 * jnp.sum(rb[...].astype(F32), axis=0)
    shared = pair_sum(jnp.sum(embed * d_embed, axis=1, keepdims=True))
    pool_s[...] = (d_embed - embed * shared) / pnorm / counts
    dn_s[...] = jnp.zeros_like(dn_s)
    for k in range(8):
        dn = pool_s[2 * k : 2 * k + 2, :] * gain[0:1, chunk(k)]
        dh, dm, dl = split3(dn)
        dn_s[0:2, chunk(k)] = dh
        dn_s[2:4, chunk(k)] = dm
        dn_s[4:6, chunk(k)] = dl
        dn_s[8:10, chunk(k)] = dn
    dn3 = jnp.where(row16 < 6, dn_s[...], 0.0).astype(BF16)

    s3 = mm(dn3, hv[...], NT)
    s0 = s3[0:1] + s3[2:3] + s3[4:5]
    s1 = s3[1:2] + s3[3:4] + s3[5:6]
    s = jnp.where(inside0, s0, jnp.where(inside1, s1, 0.0))
    b = rstd * rstd * rstd * s * (1.0 / width)
    u3 = mm(up[...], dn3, NT)
    u0 = u3[:, 0:1] + u3[:, 2:3] + u3[:, 4:5]
    u1 = u3[:, 1:2] + u3[:, 3:4] + u3[:, 5:6]
    blt = (2.0 * (u0 * w0 + u1 * w1 - b * hut)).astype(BF16)
    tiles_down, tiles_up = feat // 128, width // 128
    per = (tiles_down + tiles_up) // nq

    def put(t, x):
        ab[t // per, :, (t % per) * 128 : (t % per) * 128 + 128] = x

    def get(ref, t):
        return ref[t // per, :, (t % per) * 128 : (t % per) * 128 + 128]

    down_part = mm(blt, av[...])
    for t in range(tiles_down):
        put(t, down_part[:, t * 128 : t * 128 + 128])
    fl = flt.astype(F32)
    fb = b * fl
    fbh = fb.astype(BF16)
    fbl = (fb - fbh.astype(F32)).astype(BF16)
    f0 = jnp.sum(w0 * fl, axis=1, keepdims=True)
    f1 = jnp.sum(w1 * fl, axis=1, keepdims=True)
    fb2 = jnp.concatenate([fbh, fbl], axis=0)
    for k in range(8):
        up2 = mm(fb2, hv[:, chunk(k)])
        up2 = up2[0:16] + up2[16:32]
        up_part = 2.0 * (f0 * dn_s[8:9, chunk(k)] + f1 * dn_s[9:10, chunk(k)] - up2)
        for t in range(wc // 128):
            put(tiles_down + k * (wc // 128) + t, up_part[:, t * 128 : t * 128 + 128])

    def half(which):
        return pl.ds(pl.multiple_of(8 * which, 8), 8)

    other = 1 - core
    swap = pltpu.make_async_remote_copy(
        src_ref=ab.at[:, half(other), :],
        dst_ref=core_in,
        send_sem=c_send,
        recv_sem=c_recv,
        device_id=(grp, 2 * q_me + other),
        device_id_type=MESH,
    )
    swap.start()

    swap.wait_recv()
    mine = half(core)
    core_in[...] = core_in[...] + ab[:, mine, :]
    plane_in[q_me] = core_in[q_me]
    fan_out(nq, plane_peer, lambda there: core_in.at[there], plane_in, q_me, p_sems)
    w_step5()

    row_id = iota((128, tok), 0)
    col_s[...] = jnp.transpose(jnp.where(row_id == 0, w0 + w1, jnp.where(row_id == 1, b, 0.0)))
    blf = jnp.concatenate([blt.astype(F32), jnp.zeros((112, tok), F32)], axis=0)
    bl_s[...] = jnp.transpose(blf).astype(BF16)

    def rows_dy(i, carry):
        rows = pl.ds(pl.multiple_of(i * 16, 16), 16)
        c = col_s[rows, :]
        second = jnp.where(i * 16 >= offsets[1], 1, 0)
        dn_row = dn_s[pl.ds(8 + second, 1), :]
        dyv[rows, :] = (c[:, 0:1] * dn_row - c[:, 1:2] * hv[rows, :].astype(F32)).astype(BF16)
        return carry

    lax.fori_loop(0, tok // 16, rows_dy, 0, unroll=2)

    fan_wait(nq, plane_in, p_sems)
    z_in[grp] = jnp.sum(plane_in[...], axis=0)
    fan_out(ng, z_peer, lambda there: z_in.at[grp], z_in, grp, z_sems)
    w_step6()

    fan_wait(nl, rub, v_sems)
    d_unit = 50.0 * jnp.sum(rub[...].astype(F32), axis=0)
    unit = unit_s[...]
    unit_s[...] = (d_unit - unit * pair_sum(jnp.sum(unit * d_unit, axis=1, keepdims=True))) / qnorm
    for k in range(8):
        query_s[:, chunk(k)] = unit_s[2 * k : 2 * k + 2, :]
    stored = [store(query_s, query_out, 10)]
    fan_wait(nq, ll, l_sems)
    loss_s[...] = jnp.sum(ll[...], axis=0)[0:1, 0:1] * (1.0 / passages)
    stored.append(store(loss_s, loss_out, 11))
    w_finish(4 * y_me + x_me + 1 - 2 * lax.rem(x_me, 2))
    tile_start(1)
    tile(0, 0)
    tile_start(2)
    tile(1, 0)

    fan_wait(ng, z_in, z_sems)
    total_s[q_me, mine, :] = jnp.sum(z_in[...], axis=0)

    def gather_piece(o, carry):
        there, device = plane_peer(o)
        pltpu.make_async_remote_copy(
            src_ref=total_s.at[q_me, mine, :],
            dst_ref=total_s.at[q_me, mine, :],
            send_sem=g_sems.at[0],
            recv_sem=g_sems.at[1],
            device_id=device,
            device_id_type=MESH,
        ).start()
        return carry

    lax.fori_loop(1, nq, gather_piece, 0)
    tile_start(3)
    tile(2, 0)
    tile_start(4)
    tile(3, 0)
    amount(total_s.at[0 : nq - 1, mine, :], g_sems).wait_recv()
    back = pltpu.make_async_remote_copy(
        src_ref=total_s.at[:, mine, :],
        dst_ref=total_s.at[:, mine, :],
        send_sem=s_send,
        recv_sem=s_recv,
        device_id=(grp, 2 * q_me + other),
        device_id_type=MESH,
    )
    back.start()

    def tiles(t, carry):
        tile_start(t + 1)
        return tile(t, carry)

    lax.fori_loop(4, 7, tiles, 0)
    tile(7, 0)

    back.wait_recv()
    for t in range(tiles_down):
        down_s[:, t * 128 : t * 128 + 128] = get(total_s, t)
    for t in range(tiles_up):
        up_s[:, t * 128 : t * 128 + 128] = get(total_s, tiles_down + t)
    stored.append(store(down_s, down_out, 12))
    stored.append(store(up_s, up_out, 13))
    fan_drain(nl, ub, u_sems)
    fan_drain(nq, eb, e_sems)
    fan_drain(nl, lx, x_sems)
    fan_drain(nq, dpb, d_sems)
    fan_drain(nq, ll, l_sems)
    fan_drain(nl, dub, v_sems)
    fan_drain(nq, core_in, p_sems)
    fan_drain(ng, z_in, z_sems)
    amount(total_s.at[0 : nq - 1, mine, :], g_sems).wait_send()
    swap.wait_send()
    back.wait_send()
    w_drain()
    lax.fori_loop(0, 8, tile_stored, 0)
    for copy in stored:
        copy.wait()


def finish(*refs):
    sources, targets, stages, sems = refs[0:5], refs[5:10], refs[10:15], refs[15]
    rows = sources[0].shape[0] // 8
    pieces = [(0, pl.ds(i * rows, rows)) for i in range(8)]
    pieces += [(k, slice(None)) for k in range(1, 5)]
    arriving = [
        pltpu.make_async_copy(sources[k].at[part, :], stages[k].at[part, :], sems.at[0, i])
        for i, (k, part) in enumerate(pieces)
    ]
    leaving = [
        pltpu.make_async_copy(stages[k].at[part, :], targets[k].at[part, :], sems.at[1, i])
        for i, (k, part) in enumerate(pieces)
    ]
    for copy in arriving:
        copy.start()
    for first, then in zip(arriving, leaving):
        first.wait()
        then.start()
    for copy in leaving:
        copy.wait()


def per_device(ng, nq, attn, hidden, weight, down, up, gain, queries, lengths, offsets, positives):
    tok, width = hidden.shape
    feat = attn.shape[1]
    wc = width // 8
    nl = 2 * ng
    piece = (feat + width) // nq
    hbm = pl.BlockSpec(memory_space=pltpu.HBM)
    dma = pltpu.SemaphoreType.DMA
    outs = (
        jax.ShapeDtypeStruct((tok, feat), BF16),
        jax.ShapeDtypeStruct((2, width), F32),
        jax.ShapeDtypeStruct((16, feat), F32),
        jax.ShapeDtypeStruct((16, width), F32),
        jax.ShapeDtypeStruct((1, 1), F32),
    )
    stages = [pltpu.VMEM(out.shape, out.dtype) for out in outs]
    results = pl.pallas_call(
        functools.partial(kernel, ng, nq),
        out_shape=outs,
        in_specs=[hbm] * 10,
        out_specs=(hbm,) * 5,
        scratch_shapes=[
            pltpu.VMEM((tok, width), BF16),
            pltpu.VMEM((tok, feat), BF16),
            pltpu.VMEM((2 * nq, 64, width), BF16),
            pltpu.VMEM((tok, width), BF16),
            *stages,
            pltpu.VMEM((16, feat), BF16),
            pltpu.VMEM((16, width), BF16),
            pltpu.VMEM((1, width), F32),
            pltpu.VMEM((2, width), BF16),
            pltpu.SMEM((2,), jnp.int32),
            pltpu.SMEM((2,), jnp.int32),
            pltpu.SMEM((2,), jnp.int32),
            pltpu.VMEM((nl, 16, wc + 128), BF16),
            pltpu.VMEM((nq, 16, wc), BF16),
            pltpu.VMEM((16, wc), F32),
            pltpu.VMEM((16, wc), F32),
            pltpu.VMEM((tok, 128), F32),
            pltpu.VMEM((tok, 128), F32),
            pltpu.VMEM((tok, 128), BF16),
            pltpu.VMEM((16, width), F32),
            pltpu.VMEM((nl, 8, 128), F32),
            pltpu.VMEM((nq, 8, 128), F32),
            pltpu.VMEM((nq, 16, wc), BF16),
            pltpu.VMEM((nq, 16, wc), BF16),
            pltpu.VMEM((nl, 16, wc), BF16),
            pltpu.VMEM((nl, 16, wc), BF16),
            pltpu.VMEM((nq, 16, piece), F32),
            pltpu.VMEM((nq, 8, piece), F32),
            pltpu.VMEM((nq, 8, piece), F32),
            pltpu.VMEM((ng, 8, piece), F32),
            pltpu.VMEM((nq, 16, piece), F32),
            dma((14,)),
            dma((8,)),
            dma((2,)),
            dma((2,)),
            dma((2,)),
            dma((2,)),
            dma((2,)),
            dma((2,)),
            dma,
            dma,
            dma((2,)),
            dma((2,)),
            dma((2,)),
            dma,
            dma,
            dma((2,)),
            dma((2, 3, nq)),
            dma,
            dma((nq,)),
            dma,
            dma((2, nq)),
        ],
        compiler_params=pltpu.CompilerParams(
            collective_id=0, has_side_effects=True, vmem_limit_bytes=56 * 1024 * 1024
        ),
    )(hidden, attn, weight, down.T, up, gain.reshape(1, width), queries, lengths, offsets, positives)
    attention, query, down_sum, up_sum, loss = pl.pallas_call(
        finish,
        out_shape=outs,
        in_specs=[hbm] * 5,
        out_specs=(hbm,) * 5,
        scratch_shapes=[*stages, dma((2, 12))],
    )(*results)
    return attention, query, down_sum.T, up_sum, loss.reshape(())


def solution(mesh):
    ng = mesh.shape["grp"]
    nq = mesh.shape["dp"] // 2
    both = P(("grp", "dp"))
    rows = P(("grp", "dp"), None)
    return jax.shard_map(
        functools.partial(per_device, ng, nq),
        mesh=mesh,
        in_specs=(rows, rows, P("dp", None), P(), P(), P(), rows, both, both, both),
        out_specs=(rows, rows, P(), P(), P()),
        check_vma=False,
    )
```
